256 devices in a mesh: cls: 4 (over x_lo, core), row: 64 (over x_hi, z, y).
Axes of the slice: x: 4 (x_hi: 2, x_lo: 2; x = x_hi * 2 + x_lo), y: 4, z: 8, core: 2. Of those that a mesh axis runs over, the one named last changes fastest.
Arguments:
- scores: float32 [16384, 64], P('row', 'cls'), may hold values from -30 to 280
- labels: int32 [16384], P('row'), may hold values from 0 to 63
- nodes: int32 [16384, 64], P('row', 'cls'), may hold values from 0 to 3
- bins: int32 [16384, 256], P('row'), may hold values from 0 to 127
- pick_feature: int32 [64, 4], P('cls'), may hold values from 0 to 255
- pick_bin: int32 [64, 4], P('cls'), may hold values from 0 to 126
Outputs:
- best_gain: float32 [64, 4], P('cls')
- new_scores: float32 [16384, 64], P('row', 'cls')
The draws below stay inside these ranges and needn't reach their ends.
All inputs are finite; a program needn't handle non-finite values.
Results may differ from the reference program's by a relative error of at most 0.0014.
Values sent between devices are 32-bit elements; how exact they have to be, the bound alone decides.
No kernel may reach another device: no remote copies, remote signals or barrier semaphores. Data moves between devices by JAX's collectives and lax.ppermute only.
A program may use at most 128 MiB of HBM per device.

```python
import jax
import jax.numpy as jnp
from jax import lax

CLASSES = 64
FEATURES = 256
BINS = 128
NODES = 4
ROWS = 16384


def draw_scores(key, part):
    key_base = jax.random.fold_in(key, 0)
    base = jax.random.normal(key_base, (ROWS, CLASSES), jnp.float32)
    class_range = jnp.arange(CLASSES, dtype=jnp.int32)
    ramp = 1.1 * class_range.astype(jnp.float32) / (CLASSES - 1)
    value = jnp.clip(2.0 * base, -8.0, 8.0) + ramp
    return value


def plant(array, stream_key, low, largest):
    longest = array.shape.index(max(array.shape))
    spots = []
    for shift in (0, 1):
        where = [jax.random.randint(jax.random.fold_in(stream_key, axis), (), 0, length) for axis, length in enumerate(array.shape)]
        where[longest] = (where[longest] + shift) % array.shape[longest]
        spots.append(tuple(where))
    return array.at[spots[0]].set(low).at[spots[1]].set(largest)


def setup_inputs(seed: int = 0) -> dict:
    seeds = jax.random.split(jax.random.key(seed), 7)
    scores = draw_scores(jax.random.fold_in(seeds[6], 71), 0)
    labels = plant(jax.random.randint(seeds[1], (ROWS,), 0, CLASSES), jax.random.fold_in(seeds[1], 1), 0, CLASSES - 1).astype(jnp.int32)
    nodes = plant(jax.random.randint(seeds[2], (ROWS, CLASSES), 0, NODES), jax.random.fold_in(seeds[2], 1), 0, NODES - 1).astype(jnp.int32)
    bins = plant(jax.random.randint(seeds[3], (ROWS, FEATURES), 0, BINS), jax.random.fold_in(seeds[3], 1), 0, BINS - 1).astype(jnp.int32)
    pick_feature = plant(jax.random.randint(seeds[4], (CLASSES, NODES), 0, FEATURES), jax.random.fold_in(seeds[4], 1), 0, FEATURES - 1).astype(jnp.int32)
    pick_bin = plant(jax.random.randint(seeds[5], (CLASSES, NODES), 0, BINS - 1), jax.random.fold_in(seeds[5], 1), 0, (BINS - 1) - 1).astype(jnp.int32)
    return dict(scores=scores, labels=labels, nodes=nodes, bins=bins, pick_feature=pick_feature, pick_bin=pick_bin)


reg_lambda = 1.0
learn_rate = 0.5


def reference(scores, labels, nodes, bins, pick_feature, pick_bin):
    highest = jnp.max(scores, axis=1, keepdims=True)
    exponent = jnp.exp(scores - highest)
    prob = exponent / jnp.sum(exponent, axis=1, keepdims=True)
    class_range = jnp.arange(CLASSES, dtype=jnp.int32)
    target = (labels[:, None] == class_range[None, :]).astype(jnp.float32)
    gradient = lax.optimization_barrier((prob - target).astype(jnp.bfloat16)).astype(jnp.float32)
    hessian = lax.optimization_barrier((2.0 * prob * (1.0 - prob)).astype(jnp.bfloat16)).astype(jnp.float32)
    node_mask = nodes[:, :, None] == jnp.arange(NODES, dtype=jnp.int32)[None, None, :]
    paired = jnp.stack([jnp.where(node_mask, gradient[:, :, None], 0.0),
                        jnp.where(node_mask, hessian[:, :, None], 0.0)], axis=-1)
    paired = paired.reshape(ROWS, CLASSES * NODES * 2)
    bin_hot = (jnp.arange(BINS, dtype=jnp.int32)[:, None, None] == pick_bin[None, :, :]).astype(jnp.float32)

    def per_feature(carry, inputs):
        column, index = inputs
        hist = jax.ops.segment_sum(paired, column, num_segments=BINS).reshape(BINS, CLASSES, NODES, 2)
        running = jnp.cumsum(hist, axis=0)
        grad_total = running[-1:, :, :, 0]
        hess_total = running[-1:, :, :, 1]
        grad_left = running[:-1, :, :, 0]
        hess_left = running[:-1, :, :, 1]
        gain = 0.5 * (grad_left * grad_left / (hess_left + reg_lambda)
                      + (grad_total - grad_left) ** 2 / (hess_total - hess_left + reg_lambda)
                      - grad_total * grad_total / (hess_total + reg_lambda))
        best, stats = carry
        best = jnp.maximum(best, jnp.max(gain, axis=0))
        at_pick = jnp.sum(running * bin_hot[:, :, :, None], axis=0)
        stacked = jnp.concatenate([at_pick, running[-1]], axis=-1)
        chosen = (pick_feature == index)[:, :, None]
        stats = stats + jnp.where(chosen, stacked, 0.0)
        return (best, stats), None

    initial = (jnp.full((CLASSES, NODES), -1e30, jnp.float32), jnp.zeros((CLASSES, NODES, 4), jnp.float32))
    (best_gain, stats), unused = lax.scan(per_feature, initial,
                                          (bins.T, jnp.arange(FEATURES, dtype=jnp.int32)))
    left_weight = -stats[:, :, 0] / (stats[:, :, 1] + reg_lambda)
    right_weight = -(stats[:, :, 2] - stats[:, :, 0]) / (stats[:, :, 3] - stats[:, :, 1] + reg_lambda)
    row_feature = jnp.sum(jnp.where(node_mask, pick_feature[None, :, :], 0), axis=2).astype(jnp.int32)
    row_bin = jnp.sum(jnp.where(node_mask, pick_bin[None, :, :], 0), axis=2).astype(jnp.int32)
    row_left = jnp.sum(jnp.where(node_mask, left_weight[None, :, :], 0.0), axis=2)
    row_right = jnp.sum(jnp.where(node_mask, right_weight[None, :, :], 0.0), axis=2)
    value_at = jnp.take_along_axis(bins, row_feature, axis=1)
    leaf = jnp.where(value_at <= row_bin, row_left, row_right)
    return best_gain, scores + learn_rate * leaf
```

```python
import jax
import jax.numpy as jnp
from jax import lax
from jax.experimental import pallas as pl
from jax.experimental.pallas import tpu as pltpu
from jax.sharding import Mesh, PartitionSpec as P

BINS = 128
NODES = 4
SHARD = 16
HALF = 128
GROUPS = 32
FEATS = 8
PART = 8

reg_lambda = 1.0
learn_rate = 0.5

CLS = ("xl", "core")
ROW = ("xh", "z", "y")
VMEM = pl.BlockSpec(memory_space=pltpu.VMEM)
SMEM = pl.BlockSpec(memory_space=pltpu.SMEM)


def params(mib):
    return pltpu.CompilerParams(vmem_limit_bytes=mib * 1024 * 1024)


def prepare_kernel(place, every, labels, bins, send):
    xl, core = place[0], place[1]

    def half(x):
        return jnp.where(core == 0, x[..., :HALF], x[..., HALF:])

    scores = [half(every[i, :SHARD, :]) for i in range(4)]
    nodes = [half(every[i, SHARD:, :]) for i in range(4)]
    label = half(labels[...])
    top = jnp.max(jnp.maximum(jnp.maximum(scores[0], scores[1]), jnp.maximum(scores[2], scores[3])), axis=0, keepdims=True)
    exponent = [jnp.exp(s - top) for s in scores]
    denominator = jnp.sum((exponent[0] + exponent[1]) + (exponent[2] + exponent[3]), axis=0, keepdims=True)
    prob = [jnp.where(xl == 0, exponent[i], exponent[2 + i]) / denominator for i in range(2)]
    node = [jnp.where(xl == 0, nodes[i], nodes[2 + i]) for i in range(2)]
    columns = bins[pl.ds(pl.multiple_of(core * HALF, HALF), HALF), :].astype(jnp.float32).T
    label_rows = jnp.broadcast_to(label, (8, HALF))
    for q in range(2):
        part = slice(q * PART, (q + 1) * PART)
        for group in range(GROUPS):
            where = q * GROUPS + group
            send[where, 0:8] = prob[0][part]
            send[where, 8:16] = prob[1][part]
            send[where, 16:24] = node[0][part]
            send[where, 24:32] = node[1][part]
            send[where, 32:40] = columns[group * FEATS : (group + 1) * FEATS]
            send[where, 40:48] = label_rows


def route_kernel(picks, nodes, bins, route):
    pick = picks[...]
    column = jnp.concatenate([pick[:, n : n + 1] for n in range(NODES)], axis=0)
    features = bins.shape[1]
    hot = (lax.broadcasted_iota(jnp.int32, (NODES * SHARD, features), 1) == (column // BINS)).astype(jnp.bfloat16)
    value = lax.dot_general(
        hot, bins[...].astype(jnp.bfloat16), (((1,), (1,)), ((), ())), preferred_element_type=jnp.float32
    )
    right = (value > (column % BINS).astype(jnp.float32)).astype(jnp.int32)
    node = nodes[...]
    out = 2 * node
    for n in range(NODES):
        out = out + jnp.where(node == n, right[n * SHARD : (n + 1) * SHARD], 0)
    route[...] = out


CHUNK = 8


def left_kernel(place, taken, left, paired, mask):
    xl, quarter = place[0], place[2]
    lane_class = lax.broadcasted_iota(jnp.int32, (PART, HALF), 0) + quarter * PART
    ids = [(lane_class + (2 * xl + shard) * SHARD).astype(jnp.float32) for shard in range(2)]
    bin_range = lax.broadcasted_iota(jnp.int32, (BINS, HALF), 0).astype(jnp.bfloat16)
    one, zero = jnp.ones((), jnp.bfloat16), jnp.zeros((), jnp.bfloat16)

    @pl.loop(0, taken.shape[0] // CHUNK)
    def _(chunk):
        for step in range(CHUNK):
            source = chunk * CHUNK + step
            lanes = slice(step * HALF, (step + 1) * HALF)
            label = taken[source, 40:48]
            for shard in range(2):
                prob = taken[source, shard * 8 : shard * 8 + 8]
                node = taken[source, 16 + shard * 8 : 24 + shard * 8]
                target = (label == ids[shard]).astype(jnp.float32)
                values = ((prob - target), 2.0 * prob * (1.0 - prob))
                for pair in range(2):
                    tile = jnp.concatenate([jnp.where(node == float(n), values[pair], 0.0) for n in range(NODES)], axis=0)
                    first = shard * 64 + pair * 32
                    paired[first : first + 32, lanes] = tile.astype(jnp.bfloat16)
            for f in range(FEATS):
                row = jnp.broadcast_to(taken[source, 32 + f : 33 + f], (BINS, HALF)).astype(jnp.bfloat16)
                mask[f * BINS : (f + 1) * BINS, lanes] = jnp.where(bin_range >= row, one, zero)
        product = lax.dot_general(
            paired[...], mask[...], (((1,), (1,)), ((), ())), preferred_element_type=jnp.float32
        )

        @pl.when(chunk == 0)
        def _():
            left[...] = product

        @pl.when(chunk > 0)
        def _():
            left[...] += product


def gain_kernel(place, own, other, target, spread):
    group = place[3]
    rows = NODES * PART
    grad = own[:rows] + other[:rows]
    hess = own[rows:] + other[rows:]
    pick = target[...] - group * (FEATS * BINS)
    lane = lax.broadcasted_iota(jnp.int32, (rows, BINS), 1)
    best = None
    sums = [jnp.zeros((rows, BINS), jnp.float32) for _ in range(2)]
    totals = [jnp.zeros((rows, 1), jnp.float32) for _ in range(2)]
    for f in range(FEATS):
        g = grad[:, f * BINS : (f + 1) * BINS]
        h = hess[:, f * BINS : (f + 1) * BINS]
        gt = g[:, BINS - 1 :]
        ht = h[:, BINS - 1 :]
        gain = 0.5 * (g * g / (h + reg_lambda) + (gt - g) ** 2 / (ht - h + reg_lambda) - gt * gt / (ht + reg_lambda))
        gain = jnp.where(lane == BINS - 1, -jnp.inf, gain)
        best = gain if best is None else jnp.maximum(best, gain)
        here = lane + f * BINS == pick
        inside = (pick >= f * BINS) & (pick < (f + 1) * BINS)
        for i, (x, t) in enumerate(((g, gt), (h, ht))):
            sums[i] = jnp.where(here, x, sums[i])
            totals[i] = jnp.where(inside, t, totals[i])
    columns = [
        jnp.max(best, axis=1, keepdims=True),
        jnp.sum(sums[0], axis=1, keepdims=True),
        jnp.sum(sums[1], axis=1, keepdims=True),
        totals[0],
        totals[1],
    ]
    lane8 = lax.broadcasted_iota(jnp.int32, (PART, BINS), 1)
    tile = jnp.zeros((PART, BINS), jnp.float32)
    for j, column in enumerate(columns):
        for n in range(NODES):
            tile = jnp.where(lane8 == j * NODES + n, column[n * PART : (n + 1) * PART], tile)
    spread[...] = jnp.broadcast_to(tile[None], spread.shape)


def finish_kernel(gathered, scores, route, best, new_scores):
    top, total = [], []
    for q in range(2):
        block = gathered[q * GROUPS : (q + 1) * GROUPS]
        top.append(jnp.max(block, axis=0))
        total.append(jnp.sum(block, axis=0))
    top = jnp.concatenate(top, axis=0)
    total = jnp.concatenate(total, axis=0)
    best[...] = top.T[:NODES, :SHARD]
    grad_left, hess_left, grad_total, hess_total = (total[:, 4 * j : 4 * j + 4] for j in range(1, 5))
    left = -grad_left / (hess_left + reg_lambda)
    right = -(grad_total - grad_left) / (hess_total - hess_left + reg_lambda)
    way = route[...]
    leaf = jnp.zeros(way.shape, jnp.float32)
    for n in range(NODES):
        leaf = jnp.where(way == 2 * n, left[:, n : n + 1], leaf)
        leaf = jnp.where(way == 2 * n + 1, right[:, n : n + 1], leaf)
    new_scores[...] = scores[...] + learn_rate * leaf


def per_device(scores, labels, nodes, bins, pick_feature, pick_bin):
    xl, core, xh = (lax.axis_index(a) for a in ("xl", "core", "xh"))
    group = lax.axis_index("z") * lax.axis_size("y") + lax.axis_index("y")
    place = jnp.stack([xl, core, xh, group]).astype(jnp.int32)
    chips = 2 * GROUPS
    scores_t, nodes_t = scores.T, nodes.T
    picks = pick_feature * BINS + pick_bin
    f32 = jnp.float32

    every = lax.all_gather(jnp.concatenate([scores_t, nodes_t.astype(f32)], axis=0), CLS)
    send = pl.pallas_call(
        prepare_kernel,
        out_shape=jax.ShapeDtypeStruct((chips, 48, HALF), f32),
        in_specs=[SMEM, VMEM, VMEM, VMEM],
        out_specs=VMEM,
        compiler_params=params(16),
        name="prepare",
    )(place, every, labels.astype(f32)[None], bins)
    route = pl.pallas_call(
        route_kernel,
        out_shape=jax.ShapeDtypeStruct((SHARD, 2 * HALF), jnp.int32),
        in_specs=[VMEM] * 3,
        out_specs=VMEM,
        compiler_params=params(16),
        name="route",
    )(picks, nodes_t, bins)
    taken = lax.all_to_all(send, ROW, 0, 0)
    left = pl.pallas_call(
        left_kernel,
        out_shape=jax.ShapeDtypeStruct((128, FEATS * BINS), f32),
        in_specs=[SMEM, VMEM],
        out_specs=VMEM,
        scratch_shapes=[
            pltpu.VMEM((128, CHUNK * HALF), jnp.bfloat16),
            pltpu.VMEM((FEATS * BINS, CHUNK * HALF), jnp.bfloat16),
        ],
        compiler_params=params(32),
        name="left",
    )(place, taken)
    halves = left.reshape(2, 64, FEATS * BINS)
    own = lax.dynamic_index_in_dim(halves, core, 0, keepdims=False)
    away = lax.dynamic_index_in_dim(halves, 1 - core, 0, keepdims=False)
    other = lax.ppermute(away, "core", [(0, 1), (1, 0)])
    target = lax.dynamic_slice_in_dim(picks, xh * PART, PART, 0).T.reshape(NODES * PART, 1)
    spread = pl.pallas_call(
        gain_kernel,
        out_shape=jax.ShapeDtypeStruct((chips, PART, BINS), f32),
        in_specs=[SMEM, VMEM, VMEM, VMEM],
        out_specs=VMEM,
        compiler_params=params(16),
        name="gain",
    )(place, own, other, target)
    gathered = lax.all_to_all(spread, ROW, 0, 0)
    best, new_scores = pl.pallas_call(
        finish_kernel,
        out_shape=(jax.ShapeDtypeStruct((NODES, SHARD), f32), jax.ShapeDtypeStruct((SHARD, 2 * HALF), f32)),
        in_specs=[VMEM] * 3,
        out_specs=(VMEM, VMEM),
        compiler_params=params(16),
        name="finish",
    )(gathered, scores_t, route)
    return best.T, new_scores.T


def solution(mesh):
    fine = Mesh(mesh.devices.reshape(2, 2, 2, 8, 4), CLS + ROW)
    in_specs = (P(ROW, CLS), P(ROW), P(ROW, CLS), P(ROW, None), P(CLS, None), P(CLS, None))
    out_specs = (P(CLS, None), P(ROW, CLS))
    return jax.shard_map(per_device, mesh=fine, in_specs=in_specs, out_specs=out_specs, check_vma=False)
```

```python
import jax
import jax.numpy as jnp
from jax import lax
from jax.experimental import pallas as pl
from jax.experimental.pallas import tpu as pltpu
from jax.sharding import Mesh, PartitionSpec as P

BINS = 128
NODES = 4
SHARD = 16
HALF = 128
PART = 8
FEATS = 8
LAYERS = 8
COLUMNS = 4
BLOCK = 4 * PART + FEATS
PEERS = 2 * COLUMNS

reg_lambda = 1.0
learn_rate = 0.5

CLS = ("xl", "core")
ROW = ("xh", "z", "y")
VMEM = pl.BlockSpec(memory_space=pltpu.VMEM)
SMEM = pl.BlockSpec(memory_space=pltpu.SMEM)
BF16 = jnp.bfloat16
F32 = jnp.float32
LAST_DIMS = (((1,), (1,)), ((), ()))


def params(mib):
    return pltpu.CompilerParams(vmem_limit_bytes=mib * 1024 * 1024)


def call(kernel, name, shapes, specs, args, scratch=(), mib=16):
    many = isinstance(shapes, tuple)
    return pl.pallas_call(
        kernel,
        out_shape=shapes,
        in_specs=specs,
        out_specs=(VMEM,) * len(shapes) if many else VMEM,
        scratch_shapes=list(scratch),
        compiler_params=params(mib),
        name=name,
    )(*args)


def join_kernel(scores, nodes, joined):
    joined[:SHARD] = scores[...]
    joined[SHARD:] = nodes[...].astype(F32)


def prepare_kernel(place, every, labels, bins, send, columns, sem):
    xl, core = place[0], place[1]
    start = pl.multiple_of(core * HALF, HALF)
    fetch = pltpu.make_async_copy(bins.at[pl.ds(start, HALF), :], columns, sem)
    fetch.start()

    def half(x):
        return jnp.where(core == 0, x[..., :HALF], x[..., HALF:])

    scores = [half(every[i, :SHARD, :]) for i in range(4)]
    nodes = [half(every[i, SHARD:, :]) for i in range(4)]
    label = half(labels[...]).astype(F32)
    top = jnp.max(jnp.maximum(jnp.maximum(scores[0], scores[1]), jnp.maximum(scores[2], scores[3])), axis=0, keepdims=True)
    exponent = [jnp.exp(s - top) for s in scores]
    denominator = jnp.sum((exponent[0] + exponent[1]) + (exponent[2] + exponent[3]), axis=0, keepdims=True)
    label_rows = jnp.broadcast_to(label, (8, HALF))
    common = []
    for i in range(2):
        common.append(jnp.where(xl == 0, exponent[i], exponent[2 + i]) / denominator)
    for i in range(2):
        common.append(jnp.where(xl == 0, nodes[i], nodes[2 + i]))
    for layer in range(LAYERS):
        for i in range(4):
            send[layer, i * SHARD : (i + 1) * SHARD] = common[i]
        send[layer, 96:104] = label_rows
    fetch.wait()
    turned = columns[...].astype(F32).T
    width = COLUMNS * FEATS
    for layer in range(LAYERS):
        send[layer, 64:96] = turned[layer * width : (layer + 1) * width]


def relay_kernel(came, send):
    for layer in range(LAYERS):
        for q in range(2):
            parts = [came[layer, i * SHARD + q * PART : i * SHARD + (q + 1) * PART] for i in range(4)]
            for y in range(COLUMNS):
                for i in range(4):
                    row = layer * BLOCK + i * PART
                    send[q * COLUMNS + y, row : row + PART] = parts[i]
        for y in range(COLUMNS):
            columns = came[layer, 64 + y * FEATS : 64 + (y + 1) * FEATS]
            for q in range(2):
                row = layer * BLOCK + 4 * PART
                send[q * COLUMNS + y, row : row + FEATS] = columns
    labels = jnp.concatenate([came[layer, 96:97] for layer in range(LAYERS)], axis=0)
    for peer in range(PEERS):
        send[peer, LAYERS * BLOCK :] = labels


def route_kernel(picks, nodes, bins, route):
    pick = picks[...]
    column = jnp.concatenate([pick[:, n : n + 1] for n in range(NODES)], axis=0)
    features = bins.shape[1]
    hot = (lax.broadcasted_iota(jnp.int32, (NODES * SHARD, features), 1) == (column // BINS)).astype(BF16)
    value = lax.dot_general(hot, bins[...].astype(BF16), LAST_DIMS, preferred_element_type=F32)
    right = (value > (column % BINS).astype(F32)).astype(jnp.int32)
    node = nodes[...]
    out = 2 * node
    for n in range(NODES):
        out = out + jnp.where(node == n, right[n * SHARD : (n + 1) * SHARD], 0)
    route[...] = out


def left_kernel(place, taken, own, away, left, *buffers):
    xl, core, quarter = place[0], place[1], place[2]
    class_id = lax.broadcasted_iota(jnp.int32, (PART, HALF), 0) + quarter * PART
    ids = [(class_id + (2 * xl + shard) * SHARD).astype(F32) for shard in range(2)]
    bin_range = lax.broadcasted_iota(jnp.int32, (BINS, HALF), 0).astype(BF16)
    one, zero = jnp.ones((), BF16), jnp.zeros((), BF16)

    def build(source, paired, mask):
        for layer in range(LAYERS):
            lanes = slice(layer * HALF, (layer + 1) * HALF)
            base = layer * BLOCK
            label = jnp.broadcast_to(taken[source, LAYERS * BLOCK + layer : LAYERS * BLOCK + layer + 1], (PART, HALF))
            tiles = []
            for shard in range(2):
                prob = taken[source, base + shard * PART : base + (shard + 1) * PART]
                node = taken[source, base + (2 + shard) * PART : base + (3 + shard) * PART]
                target = (label == ids[shard]).astype(F32)
                for value in (prob - target, 2.0 * prob * (1.0 - prob)):
                    tiles += [jnp.where(node == float(n), value, 0.0) for n in range(NODES)]
            paired[:, lanes] = jnp.concatenate(tiles, axis=0).astype(BF16)
            for f in range(FEATS):
                row = taken[source, base + 4 * PART + f : base + 4 * PART + f + 1]
                row = jnp.broadcast_to(row, (BINS, HALF)).astype(BF16)
                mask[f * BINS : (f + 1) * BINS, lanes] = jnp.where(bin_range >= row, one, zero)

    def multiply(paired, mask):
        left[...] += lax.dot_general(mask[...], paired[...], LAST_DIMS, preferred_element_type=F32)

    even, odd = buffers[:2], buffers[2:]
    left[...] = jnp.zeros_like(left)
    build(0, *even)

    @pl.loop(0, PEERS // 2)
    def _(pair):
        build(2 * pair + 1, *odd)
        multiply(*even)
        build(jnp.minimum(2 * pair + 2, PEERS - 1), *even)
        multiply(*odd)

    middle = FEATS * BINS // 2
    low = lax.broadcasted_iota(jnp.int32, (BINS, 128), 1) < 64
    for row in range(0, middle, BINS):
        a, b = left[row : row + BINS], left[middle + row : middle + row + BINS]
        first = jnp.where(low, a, pltpu.roll(b, 64, 1))
        second = jnp.where(low, pltpu.roll(a, 64, 1), b)
        own[row : row + BINS] = jnp.where(core == 0, first, second)
        away[row : row + BINS] = jnp.where(core == 0, second, first)


def gain_kernel(place, own, other, target, spread):
    group = place[3]
    lane = lax.broadcasted_iota(jnp.int32, (1, 128), 1)
    pick = target[...] - group * (FEATS * BINS) - jnp.where(lane >= 64, FEATS * BINS // 2, 0)
    line = lax.broadcasted_iota(jnp.int32, (BINS, 128), 0)
    best = jnp.full((BINS, 128), -jnp.inf, F32)
    sums = jnp.zeros((BINS, 128), F32)
    totals = jnp.zeros((1, 128), F32)
    for f in range(FEATS // 2):
        rows = slice(f * BINS, (f + 1) * BINS)
        g = own[rows] + other[rows]
        h = pltpu.roll(g, 96, 1)
        gt, ht = g[BINS - 1 :], h[BINS - 1 :]
        gain = 0.5 * (g * g / (h + reg_lambda) + (gt - g) ** 2 / (ht - h + reg_lambda) - gt * gt / (ht + reg_lambda))
        best = jnp.maximum(best, jnp.where(line == BINS - 1, -jnp.inf, gain))
        sums = jnp.where(line + f * BINS == pick, g, sums)
        inside = (pick >= f * BINS) & (pick < (f + 1) * BINS)
        totals = jnp.where(inside, gt, totals)
    best = jnp.max(best, axis=0, keepdims=True)
    sums = jnp.sum(sums, axis=0, keepdims=True)
    best = jnp.maximum(best, pltpu.roll(best, 64, 1))
    sums = sums + pltpu.roll(sums, 64, 1)
    totals = totals + pltpu.roll(totals, 64, 1)
    block = jnp.concatenate([best, jnp.where(lane < 64, sums, totals)], axis=0)
    for chip in range(spread.shape[0]):
        spread[chip] = block


def finish_kernel(gathered, scores, route, best, new_scores):
    chips = gathered.shape[0]
    weights = []
    for q in range(2):
        blocks = [gathered[chip] for chip in range(q * chips // 2, (q + 1) * chips // 2)]
        top, total = blocks[0], blocks[0]
        for block in blocks[1:]:
            top = jnp.maximum(top, block)
            total = total + block
        for n in range(NODES):
            best[n : n + 1, q * PART : (q + 1) * PART] = top[0:1, n * PART : (n + 1) * PART]
        total = total[1:2]
        gl = total
        hl, gt, ht = (pltpu.roll(total, 128 - 32 * j, 1) for j in (1, 2, 3))
        weights.append(-gl / (hl + reg_lambda))
        weights.append(-(gt - gl) / (ht - hl + reg_lambda))
    columns = jnp.concatenate(weights + [jnp.zeros((4, 128), F32)], axis=0).T
    way = route[...]
    for q in range(2):
        part = slice(q * PART, (q + 1) * PART)
        leaf = jnp.zeros((PART, way.shape[1]), F32)
        for n in range(NODES):
            for side in range(2):
                value = columns[n * PART : (n + 1) * PART, 2 * q + side : 2 * q + side + 1]
                leaf = jnp.where(way[part] == 2 * n + side, value, leaf)
        new_scores[part] = scores[part] + learn_rate * leaf


def per_device(scores, labels, nodes, bins, pick_feature, pick_bin):
    xl, core, xh = (lax.axis_index(a) for a in ("xl", "core", "xh"))
    group = lax.axis_index("z") * COLUMNS + lax.axis_index("y")
    place = jnp.stack([xl, core, xh, group]).astype(jnp.int32)
    rows = 2 * HALF
    chips = PEERS * LAYERS
    scores_t, nodes_t = scores.T, nodes.T
    shape = lambda *s: jax.ShapeDtypeStruct(s, F32)

    joined = call(join_kernel, "join", shape(2 * SHARD, rows), [VMEM] * 2, (scores_t, nodes_t))
    every = lax.all_gather(joined, CLS)
    send = call(
        prepare_kernel, "prepare", shape(LAYERS, 104, HALF), [SMEM, VMEM, VMEM, pl.BlockSpec(memory_space=pltpu.HBM)],
        (place, every, labels[None], bins),
        scratch=[pltpu.VMEM((HALF, bins.shape[1]), jnp.int32), pltpu.SemaphoreType.DMA],
    )
    came = lax.all_to_all(send, "z", 0, 0)
    send = call(relay_kernel, "relay", shape(PEERS, LAYERS * (BLOCK + 1), HALF), [VMEM], (came,))
    taken = lax.all_to_all(send, ("xh", "y"), 0, 0)
    picks = pick_feature * BINS + pick_bin
    route = call(
        route_kernel, "route", jax.ShapeDtypeStruct((SHARD, rows), jnp.int32), [VMEM] * 3, (picks, nodes_t, bins)
    )
    target = lax.dynamic_slice_in_dim(picks, xh * PART, PART, 0).T.reshape(1, NODES * PART)
    target = jnp.tile(target, (1, 4))
    buffer = [pltpu.VMEM((128, LAYERS * HALF), BF16), pltpu.VMEM((FEATS * BINS, LAYERS * HALF), BF16)]
    half = shape(FEATS * BINS // 2, 128)
    own, away = call(
        left_kernel, "left", (half, half), [SMEM, VMEM], (place, taken),
        scratch=[pltpu.VMEM((FEATS * BINS, 128), F32)] + buffer + buffer, mib=32,
    )
    other = lax.ppermute(away, "core", [(0, 1), (1, 0)])
    spread = call(gain_kernel, "gain", shape(chips, 2, 128), [SMEM, VMEM, VMEM, VMEM], (place, own, other, target))
    gathered = lax.all_to_all(spread, ROW, 0, 0)
    best, new_scores = call(
        finish_kernel, "finish", (shape(NODES, SHARD), shape(SHARD, rows)), [VMEM] * 3, (gathered, scores_t, route)
    )
    return best.T, new_scores.T


def solution(mesh):
    fine = Mesh(mesh.devices.reshape(2, 2, 2, LAYERS, COLUMNS), CLS + ROW)
    in_specs = (P(ROW, CLS), P(ROW), P(ROW, CLS), P(ROW, None), P(CLS, None), P(CLS, None))
    out_specs = (P(CLS, None), P(ROW, CLS))
    return jax.shard_map(per_device, mesh=fine, in_specs=in_specs, out_specs=out_specs, check_vma=False)
```

```python
import jax
import jax.numpy as jnp
from jax import lax
from jax.experimental import pallas as pl
from jax.experimental.pallas import tpu as pltpu
from jax.sharding import Mesh, PartitionSpec as P

BINS = 128
NODES = 4
SHARD = 16
HALF = 128
PART = 8
FEATS = 8
LAYERS = 8
COLUMNS = 4
BLOCK = 4 * PART + FEATS
PEERS = 2 * COLUMNS

reg_lambda = 1.0
learn_rate = 0.5

CLS = ("xl", "core")
ROW = ("xh", "z", "y")
VMEM = pl.BlockSpec(memory_space=pltpu.VMEM)
HBM = pl.BlockSpec(memory_space=pltpu.HBM)
SMEM = pl.BlockSpec(memory_space=pltpu.SMEM)
BF16 = jnp.bfloat16
F32 = jnp.float32
PIN = lambda x: pltpu.with_memory_space_constraint(x, pltpu.HBM)
LAST_DIMS = (((1,), (1,)), ((), ()))


def params(mib):
    return pltpu.CompilerParams(vmem_limit_bytes=mib * 1024 * 1024)


def call(kernel, name, shapes, specs, args, scratch=(), mib=16):
    many = isinstance(shapes, tuple)
    return pl.pallas_call(
        kernel,
        out_shape=shapes,
        in_specs=specs,
        out_specs=(VMEM,) * len(shapes) if many else VMEM,
        scratch_shapes=list(scratch),
        compiler_params=params(mib),
        name=name,
    )(*args)


def join_kernel(scores, nodes, labels, bins, joined, turned, label, node_buffer, label_buffer, columns, sems):
    core = lax.axis_index("core")
    start = pl.multiple_of(core * HALF, HALF)
    copies = [
        pltpu.make_async_copy(bins.at[pl.ds(start, HALF), :], columns, sems.at[0]),
        pltpu.make_async_copy(scores, joined.at[pl.ds(0, SHARD), :], sems.at[1]),
        pltpu.make_async_copy(nodes, node_buffer, sems.at[2]),
        pltpu.make_async_copy(labels, label_buffer, sems.at[3]),
    ]
    for copy in copies:
        copy.start()
    for copy in copies:
        copy.wait()
    joined[SHARD:] = node_buffer[...].astype(F32)
    turned[...] = columns[...].astype(F32).T
    row = label_buffer[...].astype(F32)
    label[...] = jnp.broadcast_to(jnp.where(core == 0, row[:, :HALF], row[:, HALF:]), label.shape)


def prepare_kernel(every, turned, label, send):
    xl, core = lax.axis_index("xl"), lax.axis_index("core")

    def half(x):
        return jnp.where(core == 0, x[..., :HALF], x[..., HALF:])

    scores = [half(every[i, :SHARD, :]) for i in range(4)]
    nodes = [half(every[i, SHARD:, :]) for i in range(4)]
    top = jnp.max(jnp.maximum(jnp.maximum(scores[0], scores[1]), jnp.maximum(scores[2], scores[3])), axis=0, keepdims=True)
    exponent = [jnp.exp(s - top) for s in scores]
    denominator = jnp.sum((exponent[0] + exponent[1]) + (exponent[2] + exponent[3]), axis=0, keepdims=True)
    prob = [jnp.where(xl == 0, exponent[i], exponent[2 + i]) / denominator for i in range(2)]
    node = [jnp.where(xl == 0, nodes[i], nodes[2 + i]) for i in range(2)]
    width = COLUMNS * FEATS
    for layer in range(LAYERS):
        for i, part in enumerate(prob + node):
            send[layer, i * SHARD : (i + 1) * SHARD] = part
        send[layer, 64:96] = turned[layer * width : (layer + 1) * width]
        send[layer, 96:104] = label[...]


def relay_kernel(came, send):
    for layer in range(LAYERS):
        for q in range(2):
            parts = [came[layer, i * SHARD + q * PART : i * SHARD + (q + 1) * PART] for i in range(4)]
            for y in range(COLUMNS):
                for i in range(4):
                    row = layer * BLOCK + i * PART
                    send[q * COLUMNS + y, row : row + PART] = parts[i]
        for y in range(COLUMNS):
            columns = came[layer, 64 + y * FEATS : 64 + (y + 1) * FEATS]
            for q in range(2):
                row = layer * BLOCK + 4 * PART
                send[q * COLUMNS + y, row : row + FEATS] = columns
    labels = jnp.concatenate([came[layer, 96:97] for layer in range(LAYERS)], axis=0)
    for peer in range(PEERS):
        send[peer, LAYERS * BLOCK :] = labels


def route_kernel(picks, nodes, bins, route):
    pick = picks[...]
    column = jnp.concatenate([pick[:, n : n + 1] for n in range(NODES)], axis=0)
    features = bins.shape[1]
    hot = (lax.broadcasted_iota(jnp.int32, (NODES * SHARD, features), 1) == (column // BINS)).astype(BF16)
    value = lax.dot_general(hot, bins[...].astype(BF16), LAST_DIMS, preferred_element_type=F32)
    right = (value > (column % BINS).astype(F32)).astype(jnp.int32)
    node = nodes[...]
    out = 2 * node
    for n in range(NODES):
        out = out + jnp.where(node == n, right[n * SHARD : (n + 1) * SHARD], 0)
    route[...] = out


def left_kernel(taken, own, away, left, *buffers):
    xl, core, quarter = (lax.axis_index(a) for a in ("xl", "core", "xh"))
    class_id = lax.broadcasted_iota(jnp.int32, (PART, HALF), 0) + quarter * PART
    ids = [(class_id + (2 * xl + shard) * SHARD).astype(F32) for shard in range(2)]
    bin_range = lax.broadcasted_iota(jnp.int32, (BINS, HALF), 0).astype(BF16)
    one, zero = jnp.ones((), BF16), jnp.zeros((), BF16)

    def build(source, paired, mask):
        for layer in range(LAYERS):
            lanes = slice(layer * HALF, (layer + 1) * HALF)
            base = layer * BLOCK
            label = jnp.broadcast_to(taken[source, LAYERS * BLOCK + layer : LAYERS * BLOCK + layer + 1], (PART, HALF))
            tiles = []
            for shard in range(2):
                prob = taken[source, base + shard * PART : base + (shard + 1) * PART]
                node = taken[source, base + (2 + shard) * PART : base + (3 + shard) * PART]
                target = (label == ids[shard]).astype(F32)
                for value in (prob - target, 2.0 * prob * (1.0 - prob)):
                    tiles += [jnp.where(node == float(n), value, 0.0) for n in range(NODES)]
            paired[:, lanes] = jnp.concatenate(tiles, axis=0).astype(BF16)
            for f in range(FEATS):
                row = taken[source, base + 4 * PART + f : base + 4 * PART + f + 1]
                row = jnp.broadcast_to(row, (BINS, HALF)).astype(BF16)
                mask[f * BINS : (f + 1) * BINS, lanes] = jnp.where(bin_range >= row, one, zero)

    def multiply(paired, mask):
        left[...] += lax.dot_general(mask[...], paired[...], LAST_DIMS, preferred_element_type=F32)

    even, odd = buffers[:2], buffers[2:]
    left[...] = jnp.zeros_like(left)
    build(0, *even)

    @pl.loop(0, PEERS // 2)
    def _(pair):
        build(2 * pair + 1, *odd)
        multiply(*even)
        build(jnp.minimum(2 * pair + 2, PEERS - 1), *even)
        multiply(*odd)

    middle = FEATS * BINS // 2
    low = lax.broadcasted_iota(jnp.int32, (BINS, 128), 1) < 64
    for row in range(0, middle, BINS):
        a, b = left[row : row + BINS], left[middle + row : middle + row + BINS]
        first = jnp.where(low, a, pltpu.roll(b, 64, 1))
        second = jnp.where(low, pltpu.roll(a, 64, 1), b)
        own[row : row + BINS] = jnp.where(core == 0, first, second)
        away[row : row + BINS] = jnp.where(core == 0, second, first)


def gain_kernel(pick_feature, pick_bin, own, other, spread):
    quarter = lax.axis_index("xh")
    group = lax.axis_index("z") * COLUMNS + lax.axis_index("y")
    lane = lax.broadcasted_iota(jnp.int32, (1, 128), 1)
    target = jnp.zeros((1, 128), jnp.int32)
    for n in range(NODES):
        for k in range(PART):
            chosen = pick_feature[n, quarter * PART + k] * BINS + pick_bin[n, quarter * PART + k]
            target = jnp.where(lane % 32 == n * PART + k, chosen, target)
    pick = target - group * (FEATS * BINS) - jnp.where(lane >= 64, FEATS * BINS // 2, 0)
    line = lax.broadcasted_iota(jnp.int32, (BINS, 128), 0)
    best = jnp.full((BINS, 128), -jnp.inf, F32)
    sums = jnp.zeros((BINS, 128), F32)
    totals = jnp.zeros((1, 128), F32)
    for f in range(FEATS // 2):
        rows = slice(f * BINS, (f + 1) * BINS)
        g = own[rows] + other[rows]
        h = pltpu.roll(g, 96, 1)
        gt, ht = g[BINS - 1 :], h[BINS - 1 :]
        gain = 0.5 * (g * g / (h + reg_lambda) + (gt - g) ** 2 / (ht - h + reg_lambda) - gt * gt / (ht + reg_lambda))
        best = jnp.maximum(best, jnp.where(line == BINS - 1, -jnp.inf, gain))
        sums = jnp.where(line + f * BINS == pick, g, sums)
        inside = (pick >= f * BINS) & (pick < (f + 1) * BINS)
        totals = jnp.where(inside, gt, totals)
    best = jnp.max(best, axis=0, keepdims=True)
    sums = jnp.sum(sums, axis=0, keepdims=True)
    best = jnp.maximum(best, pltpu.roll(best, 64, 1))
    sums = sums + pltpu.roll(sums, 64, 1)
    totals = totals + pltpu.roll(totals, 64, 1)
    block = jnp.concatenate([best, jnp.where(lane < 64, sums, totals)], axis=0)
    for chip in range(spread.shape[0]):
        spread[chip] = block


def finish_kernel(gathered, scores, route, best, new_scores):
    chips = gathered.shape[0]
    weights = []
    for q in range(2):
        blocks = [gathered[chip] for chip in range(q * chips // 2, (q + 1) * chips // 2)]
        top, total = blocks[0], blocks[0]
        for block in blocks[1:]:
            top = jnp.maximum(top, block)
            total = total + block
        for n in range(NODES):
            best[n : n + 1, q * PART : (q + 1) * PART] = top[0:1, n * PART : (n + 1) * PART]
        total = total[1:2]
        gl = total
        hl, gt, ht = (pltpu.roll(total, 128 - 32 * j, 1) for j in (1, 2, 3))
        weights.append(-gl / (hl + reg_lambda))
        weights.append(-(gt - gl) / (ht - hl + reg_lambda))
    columns = jnp.concatenate(weights + [jnp.zeros((4, 128), F32)], axis=0).T
    way = route[...]
    for q in range(2):
        part = slice(q * PART, (q + 1) * PART)
        leaf = jnp.zeros((PART, way.shape[1]), F32)
        for n in range(NODES):
            for side in range(2):
                value = columns[n * PART : (n + 1) * PART, 2 * q + side : 2 * q + side + 1]
                leaf = jnp.where(way[part] == 2 * n + side, value, leaf)
        new_scores[part] = scores[part] + learn_rate * leaf


def per_device(scores, labels, nodes, bins, pick_feature, pick_bin):
    rows = 2 * HALF
    chips = PEERS * LAYERS
    scores_t, nodes_t = scores.T, nodes.T
    shape = lambda *s: jax.ShapeDtypeStruct(s, F32)

    inputs = [PIN(x) for x in (scores_t, nodes_t, labels[None], bins)]
    joined, turned, label = call(
        join_kernel, "join", (shape(2 * SHARD, rows), shape(bins.shape[1], HALF), shape(8, HALF)), [HBM] * 4, inputs,
        scratch=[
            pltpu.VMEM((SHARD, rows), jnp.int32),
            pltpu.VMEM((1, rows), jnp.int32),
            pltpu.VMEM((HALF, bins.shape[1]), jnp.int32),
            pltpu.SemaphoreType.DMA((4,)),
        ],
    )
    every = lax.all_gather(joined, CLS)
    send = call(prepare_kernel, "prepare", shape(LAYERS, 104, HALF), [VMEM] * 3, (every, turned, label))
    came = lax.all_to_all(send, "z", 0, 0)
    send = call(relay_kernel, "relay", shape(PEERS, LAYERS * (BLOCK + 1), HALF), [VMEM], (came,))
    taken = lax.all_to_all(send, ("xh", "y"), 0, 0)
    buffer = [pltpu.VMEM((128, LAYERS * HALF), BF16), pltpu.VMEM((FEATS * BINS, LAYERS * HALF), BF16)]
    half = shape(FEATS * BINS // 2, 128)
    own, away = call(
        left_kernel, "left", (half, half), [VMEM], (taken,),
        scratch=[pltpu.VMEM((FEATS * BINS, 128), F32)] + buffer + buffer, mib=32,
    )
    other = lax.ppermute(away, "core", [(0, 1), (1, 0)])
    spread = call(
        gain_kernel, "gain", shape(chips, 2, 128), [SMEM, SMEM, VMEM, VMEM], (pick_feature.T, pick_bin.T, own, other)
    )
    pick_feature, pick_bin, spread = lax.optimization_barrier((pick_feature, pick_bin, spread))
    picks = pick_feature * BINS + pick_bin
    route = call(
        route_kernel, "route", jax.ShapeDtypeStruct((SHARD, rows), jnp.int32), [VMEM] * 3, (picks, nodes_t, bins)
    )
    gathered = lax.all_to_all(spread, ROW, 0, 0)
    best, new_scores = call(
        finish_kernel, "finish", (shape(NODES, SHARD), shape(SHARD, rows)), [VMEM] * 3, (gathered, scores_t, route)
    )
    return best.T, new_scores.T


def solution(mesh):
    fine = Mesh(mesh.devices.reshape(2, 2, 2, LAYERS, COLUMNS), CLS + ROW)
    in_specs = (P(ROW, CLS), P(ROW), P(ROW, CLS), P(ROW, None), P(CLS, None), P(CLS, None))
    out_specs = (P(CLS, None), P(ROW, CLS))
    return jax.shard_map(per_device, mesh=fine, in_specs=in_specs, out_specs=out_specs, check_vma=False)
```

```python
import jax
import jax.numpy as jnp
from jax import lax
from jax.experimental import pallas as pl
from jax.experimental.pallas import tpu as pltpu
from jax.sharding import Mesh, PartitionSpec as P

BINS = 128
NODES = 4
SHARD = 16
HALF = 128
PART = 8
FEATS = 8
LAYERS = 8
COLUMNS = 4
BLOCK = 4 * PART + FEATS
PEERS = 2 * COLUMNS

reg_lambda = 1.0
learn_rate = 0.5

CLS = ("xl", "core")
ROW = ("xh", "z", "y")
VMEM = pl.BlockSpec(memory_space=pltpu.VMEM)
HBM = pl.BlockSpec(memory_space=pltpu.HBM)
SMEM = pl.BlockSpec(memory_space=pltpu.SMEM)
BF16 = jnp.bfloat16
F32 = jnp.float32
PIN = lambda x: pltpu.with_memory_space_constraint(x, pltpu.HBM)
LAST_DIMS = (((1,), (1,)), ((), ()))


def params(mib):
    return pltpu.CompilerParams(vmem_limit_bytes=mib * 1024 * 1024)


def call(kernel, name, shapes, specs, args, scratch=(), mib=16):
    many = isinstance(shapes, tuple)
    return pl.pallas_call(
        kernel,
        out_shape=shapes,
        in_specs=specs,
        out_specs=(VMEM,) * len(shapes) if many else VMEM,
        scratch_shapes=list(scratch),
        compiler_params=params(mib),
        name=name,
    )(*args)


def join_kernel(
    scores, nodes, labels, bins, pick_feature, pick_bin, joined, turned, label, target,
    node_buffer, label_buffer, columns, picked, sems,
):
    core, quarter = lax.axis_index("core"), lax.axis_index("xh")
    start = pl.multiple_of(core * HALF, HALF)
    copies = [
        pltpu.make_async_copy(bins.at[pl.ds(start, HALF), :], columns, sems.at[0]),
        pltpu.make_async_copy(scores, joined.at[pl.ds(0, SHARD), :], sems.at[1]),
        pltpu.make_async_copy(nodes, node_buffer, sems.at[2]),
        pltpu.make_async_copy(labels, label_buffer, sems.at[3]),
        pltpu.make_async_copy(pick_feature, picked.at[0], sems.at[4]),
        pltpu.make_async_copy(pick_bin, picked.at[1], sems.at[5]),
    ]
    for copy in copies:
        copy.start()
    for copy in copies:
        copy.wait()
    joined[SHARD:] = node_buffer[...].astype(F32)
    turned[...] = columns[...].astype(F32).T
    row = label_buffer[...].astype(F32)
    label[...] = jnp.broadcast_to(jnp.where(core == 0, row[:, :HALF], row[:, HALF:]), label.shape)
    lane = lax.broadcasted_iota(jnp.int32, target.shape, 1) % (NODES * PART)
    chosen = jnp.zeros(target.shape, jnp.int32)
    for n in range(NODES):
        for k in range(PART):
            where = quarter * PART + k
            chosen = jnp.where(lane == n * PART + k, picked[0, n, where] * BINS + picked[1, n, where], chosen)
    target[...] = chosen


def prepare_kernel(every, turned, label, send):
    xl, core = lax.axis_index("xl"), lax.axis_index("core")

    def half(x):
        return jnp.where(core == 0, x[..., :HALF], x[..., HALF:])

    scores = [half(every[i, :SHARD, :]) for i in range(4)]
    nodes = [half(every[i, SHARD:, :]) for i in range(4)]
    top = jnp.max(jnp.maximum(jnp.maximum(scores[0], scores[1]), jnp.maximum(scores[2], scores[3])), axis=0, keepdims=True)
    exponent = [jnp.exp(s - top) for s in scores]
    denominator = jnp.sum((exponent[0] + exponent[1]) + (exponent[2] + exponent[3]), axis=0, keepdims=True)
    prob = [jnp.where(xl == 0, exponent[i], exponent[2 + i]) / denominator for i in range(2)]
    node = [jnp.where(xl == 0, nodes[i], nodes[2 + i]) for i in range(2)]
    width = COLUMNS * FEATS
    for layer in range(LAYERS):
        for i, part in enumerate(prob + node):
            send[layer, i * SHARD : (i + 1) * SHARD] = part
        send[layer, 64:96] = turned[layer * width : (layer + 1) * width]
        send[layer, 96:104] = label[...]


def relay_kernel(came, send):
    for layer in range(LAYERS):
        for q in range(2):
            parts = [came[layer, i * SHARD + q * PART : i * SHARD + (q + 1) * PART] for i in range(4)]
            for y in range(COLUMNS):
                for i in range(4):
                    row = layer * BLOCK + i * PART
                    send[q * COLUMNS + y, row : row + PART] = parts[i]
        for y in range(COLUMNS):
            columns = came[layer, 64 + y * FEATS : 64 + (y + 1) * FEATS]
            for q in range(2):
                row = layer * BLOCK + 4 * PART
                send[q * COLUMNS + y, row : row + FEATS] = columns
    labels = jnp.concatenate([came[layer, 96:97] for layer in range(LAYERS)], axis=0)
    for peer in range(PEERS):
        send[peer, LAYERS * BLOCK :] = labels


def route_kernel(picks, nodes, bins, route):
    pick = picks[...]
    column = jnp.concatenate([pick[:, n : n + 1] for n in range(NODES)], axis=0)
    features = bins.shape[1]
    hot = (lax.broadcasted_iota(jnp.int32, (NODES * SHARD, features), 1) == (column // BINS)).astype(BF16)
    value = lax.dot_general(hot, bins[...].astype(BF16), LAST_DIMS, preferred_element_type=F32)
    right = (value > (column % BINS).astype(F32)).astype(jnp.int32)
    node = nodes[...]
    out = 2 * node
    for n in range(NODES):
        out = out + jnp.where(node == n, right[n * SHARD : (n + 1) * SHARD], 0)
    route[...] = out


def left_kernel(taken, own, away, left, *buffers):
    xl, core, quarter = (lax.axis_index(a) for a in ("xl", "core", "xh"))
    class_id = lax.broadcasted_iota(jnp.int32, (PART, HALF), 0) + quarter * PART
    ids = [(class_id + (2 * xl + shard) * SHARD).astype(F32) for shard in range(2)]
    bin_range = lax.broadcasted_iota(jnp.int32, (BINS, HALF), 0).astype(BF16)
    one, zero = jnp.ones((), BF16), jnp.zeros((), BF16)

    def build(source, paired, mask):
        for layer in range(LAYERS):
            lanes = slice(layer * HALF, (layer + 1) * HALF)
            base = layer * BLOCK
            label = jnp.broadcast_to(taken[source, LAYERS * BLOCK + layer : LAYERS * BLOCK + layer + 1], (PART, HALF))
            tiles = []
            for shard in range(2):
                prob = taken[source, base + shard * PART : base + (shard + 1) * PART]
                node = taken[source, base + (2 + shard) * PART : base + (3 + shard) * PART]
                target = (label == ids[shard]).astype(F32)
                for value in (prob - target, 2.0 * prob * (1.0 - prob)):
                    tiles += [jnp.where(node == float(n), value, 0.0) for n in range(NODES)]
            paired[:, lanes] = jnp.concatenate(tiles, axis=0).astype(BF16)
            for f in range(FEATS):
                row = taken[source, base + 4 * PART + f : base + 4 * PART + f + 1]
                row = jnp.broadcast_to(row, (BINS, HALF)).astype(BF16)
                mask[f * BINS : (f + 1) * BINS, lanes] = jnp.where(bin_range >= row, one, zero)

    def multiply(paired, mask):
        left[...] += lax.dot_general(mask[...], paired[...], LAST_DIMS, preferred_element_type=F32)

    even, odd = buffers[:2], buffers[2:]
    left[...] = jnp.zeros_like(left)
    build(0, *even)

    @pl.loop(0, PEERS // 2)
    def _(pair):
        build(2 * pair + 1, *odd)
        multiply(*even)
        build(jnp.minimum(2 * pair + 2, PEERS - 1), *even)
        multiply(*odd)

    middle = FEATS * BINS // 2
    low = lax.broadcasted_iota(jnp.int32, (BINS, 128), 1) < 64
    for row in range(0, middle, BINS):
        a, b = left[row : row + BINS], left[middle + row : middle + row + BINS]
        first = jnp.where(low, a, pltpu.roll(b, 64, 1))
        second = jnp.where(low, pltpu.roll(a, 64, 1), b)
        own[row : row + BINS] = jnp.where(core == 0, first, second)
        away[row : row + BINS] = jnp.where(core == 0, second, first)


def gain_kernel(target, own, other, spread):
    group = lax.axis_index("z") * COLUMNS + lax.axis_index("y")
    lane = lax.broadcasted_iota(jnp.int32, (1, 128), 1)
    pick = target[:1] - group * (FEATS * BINS) - jnp.where(lane >= 64, FEATS * BINS // 2, 0)
    line = lax.broadcasted_iota(jnp.int32, (BINS, 128), 0)
    best = jnp.full((BINS, 128), -jnp.inf, F32)
    sums = jnp.zeros((BINS, 128), F32)
    totals = jnp.zeros((1, 128), F32)
    for f in range(FEATS // 2):
        rows = slice(f * BINS, (f + 1) * BINS)
        g = own[rows] + other[rows]
        h = pltpu.roll(g, 96, 1)
        gt, ht = g[BINS - 1 :], h[BINS - 1 :]
        gain = 0.5 * (g * g / (h + reg_lambda) + (gt - g) ** 2 / (ht - h + reg_lambda) - gt * gt / (ht + reg_lambda))
        best = jnp.maximum(best, jnp.where(line == BINS - 1, -jnp.inf, gain))
        sums = jnp.where(line + f * BINS == pick, g, sums)
        inside = (pick >= f * BINS) & (pick < (f + 1) * BINS)
        totals = jnp.where(inside, gt, totals)
    best = jnp.max(best, axis=0, keepdims=True)
    sums = jnp.sum(sums, axis=0, keepdims=True)
    best = jnp.maximum(best, pltpu.roll(best, 64, 1))
    sums = sums + pltpu.roll(sums, 64, 1)
    totals = totals + pltpu.roll(totals, 64, 1)
    block = jnp.concatenate([best, jnp.where(lane < 64, sums, totals)], axis=0)
    for chip in range(spread.shape[0]):
        spread[chip] = block


def finish_kernel(gathered, scores, route, best, new_scores):
    chips = gathered.shape[0]
    weights = []
    for q in range(2):
        blocks = [gathered[chip] for chip in range(q * chips // 2, (q + 1) * chips // 2)]
        top, total = blocks[0], blocks[0]
        for block in blocks[1:]:
            top = jnp.maximum(top, block)
            total = total + block
        for n in range(NODES):
            best[n : n + 1, q * PART : (q + 1) * PART] = top[0:1, n * PART : (n + 1) * PART]
        total = total[1:2]
        gl = total
        hl, gt, ht = (pltpu.roll(total, 128 - 32 * j, 1) for j in (1, 2, 3))
        weights.append(-gl / (hl + reg_lambda))
        weights.append(-(gt - gl) / (ht - hl + reg_lambda))
    columns = jnp.concatenate(weights + [jnp.zeros((4, 128), F32)], axis=0).T
    way = route[...]
    for q in range(2):
        part = slice(q * PART, (q + 1) * PART)
        leaf = jnp.zeros((PART, way.shape[1]), F32)
        for n in range(NODES):
            for side in range(2):
                value = columns[n * PART : (n + 1) * PART, 2 * q + side : 2 * q + side + 1]
                leaf = jnp.where(way[part] == 2 * n + side, value, leaf)
        new_scores[part] = scores[part] + learn_rate * leaf


def per_device(scores, labels, nodes, bins, pick_feature, pick_bin):
    rows = 2 * HALF
    chips = PEERS * LAYERS
    scores_t, nodes_t = scores.T, nodes.T
    shape = lambda *s: jax.ShapeDtypeStruct(s, F32)

    inputs = [PIN(x) for x in (scores_t, nodes_t, labels[None], bins, pick_feature.T, pick_bin.T)]
    joined, turned, label, target = call(
        join_kernel, "join",
        (
            shape(2 * SHARD, rows), shape(bins.shape[1], HALF), shape(8, HALF),
            jax.ShapeDtypeStruct((8, 128), jnp.int32),
        ),
        [HBM] * 6, inputs,
        scratch=[
            pltpu.VMEM((SHARD, rows), jnp.int32),
            pltpu.VMEM((1, rows), jnp.int32),
            pltpu.VMEM((HALF, bins.shape[1]), jnp.int32),
            pltpu.SMEM((2, NODES, SHARD), jnp.int32),
            pltpu.SemaphoreType.DMA((6,)),
        ],
    )
    every = lax.all_gather(joined, CLS)
    send = call(prepare_kernel, "prepare", shape(LAYERS, 104, HALF), [VMEM] * 3, (every, turned, label))
    came = lax.all_to_all(send, "z", 0, 0)
    send = call(relay_kernel, "relay", shape(PEERS, LAYERS * (BLOCK + 1), HALF), [VMEM], (came,))
    taken = lax.all_to_all(send, ("xh", "y"), 0, 0)
    buffer = [pltpu.VMEM((128, LAYERS * HALF), BF16), pltpu.VMEM((FEATS * BINS, LAYERS * HALF), BF16)]
    half = shape(FEATS * BINS // 2, 128)
    own, away = call(
        left_kernel, "left", (half, half), [VMEM], (taken,),
        scratch=[pltpu.VMEM((FEATS * BINS, 128), F32)] + buffer + buffer, mib=32,
    )
    other = lax.ppermute(away, "core", [(0, 1), (1, 0)])
    pick_feature, pick_bin, own = lax.optimization_barrier((pick_feature, pick_bin, own))
    picks = pick_feature * BINS + pick_bin
    route = call(
        route_kernel, "route", jax.ShapeDtypeStruct((SHARD, rows), jnp.int32), [VMEM] * 3, (picks, nodes_t, bins)
    )
    other, route = lax.optimization_barrier((other, route))
    spread = call(gain_kernel, "gain", shape(chips, 2, 128), [VMEM] * 3, (target, own, other))
    gathered = lax.all_to_all(spread, ROW, 0, 0)
    best, new_scores = call(
        finish_kernel, "finish", (shape(NODES, SHARD), shape(SHARD, rows)), [VMEM] * 3, (gathered, scores_t, route)
    )
    return best.T, new_scores.T


def solution(mesh):
    fine = Mesh(mesh.devices.reshape(2, 2, 2, LAYERS, COLUMNS), CLS + ROW)
    in_specs = (P(ROW, CLS), P(ROW), P(ROW, CLS), P(ROW, None), P(CLS, None), P(CLS, None))
    out_specs = (P(CLS, None), P(ROW, CLS))
    return jax.shard_map(per_device, mesh=fine, in_specs=in_specs, out_specs=out_specs, check_vma=False)
```

```python
import jax
import jax.numpy as jnp
from jax import lax
from jax.experimental import pallas as pl
from jax.experimental.pallas import tpu as pltpu
from jax.sharding import Mesh, PartitionSpec as P

BINS = 128
NODES = 4
SHARD = 16
HALF = 128
PART = 8
FEATS = 8
LAYERS = 8
COLUMNS = 4
BLOCK = 4 * PART + FEATS
PEERS = 2 * COLUMNS

reg_lambda = 1.0
learn_rate = 0.5

CLS = ("xl", "core")
ROW = ("xh", "z", "y")
VMEM = pl.BlockSpec(memory_space=pltpu.VMEM)
HBM = pl.BlockSpec(memory_space=pltpu.HBM)
SMEM = pl.BlockSpec(memory_space=pltpu.SMEM)
BF16 = jnp.bfloat16
F32 = jnp.float32
PIN = lambda x: pltpu.with_memory_space_constraint(x, pltpu.HBM)
LAST_DIMS = (((1,), (1,)), ((), ()))


def params(mib):
    return pltpu.CompilerParams(vmem_limit_bytes=mib * 1024 * 1024)


def call(kernel, name, shapes, specs, args, scratch=(), mib=16):
    many = isinstance(shapes, tuple)
    return pl.pallas_call(
        kernel,
        out_shape=shapes,
        in_specs=specs,
        out_specs=(VMEM,) * len(shapes) if many else VMEM,
        scratch_shapes=list(scratch),
        compiler_params=params(mib),
        name=name,
    )(*args)


def join_kernel(
    scores, nodes, labels, bins, pick_feature, pick_bin, joined, turned, label, target,
    node_buffer, label_buffer, columns, picked, sems,
):
    core, quarter = lax.axis_index("core"), lax.axis_index("xh")
    start = pl.multiple_of(core * HALF, HALF)
    copies = [
        pltpu.make_async_copy(bins.at[pl.ds(start, HALF), :], columns, sems.at[0]),
        pltpu.make_async_copy(scores, joined.at[pl.ds(0, SHARD), :], sems.at[1]),
        pltpu.make_async_copy(nodes, node_buffer, sems.at[2]),
        pltpu.make_async_copy(labels, label_buffer, sems.at[3]),
        pltpu.make_async_copy(pick_feature, picked.at[0], sems.at[4]),
        pltpu.make_async_copy(pick_bin, picked.at[1], sems.at[5]),
    ]
    for copy in copies:
        copy.start()
    for copy in copies:
        copy.wait()
    joined[SHARD:] = node_buffer[...].astype(F32)
    turned[...] = columns[...].astype(F32).T
    row = label_buffer[...].astype(F32)
    label[...] = jnp.broadcast_to(jnp.where(core == 0, row[:, :HALF], row[:, HALF:]), label.shape)
    lane = lax.broadcasted_iota(jnp.int32, target.shape, 1) % (NODES * PART)
    chosen = jnp.zeros(target.shape, jnp.int32)
    for n in range(NODES):
        for k in range(PART):
            where = quarter * PART + k
            chosen = jnp.where(lane == n * PART + k, picked[0, n, where] * BINS + picked[1, n, where], chosen)
    target[...] = chosen


def prepare_kernel(every, turned, label, send):
    xl, core, xh = (lax.axis_index(a) for a in ("xl", "core", "xh"))

    def half(x):
        return jnp.where(core == 0, x[..., :HALF], x[..., HALF:])

    scores = [half(every[i, :SHARD, :]) for i in range(4)]
    top = jnp.max(jnp.maximum(jnp.maximum(scores[0], scores[1]), jnp.maximum(scores[2], scores[3])), axis=0, keepdims=True)
    exponent = [jnp.exp(s - top) for s in scores]
    denominator = jnp.sum((exponent[0] + exponent[1]) + (exponent[2] + exponent[3]), axis=0, keepdims=True)
    parts = []
    for q in range(2):
        low = (xl == 0) == (xh == q)
        part = slice(q * PART, (q + 1) * PART)
        for shard in range(2):
            parts.append(jnp.where(low, exponent[shard][part], exponent[2 + shard][part]) / denominator)
        part = slice(SHARD + q * PART, SHARD + (q + 1) * PART)
        for shard in range(2):
            parts.append(half(jnp.where(low, every[shard, part, :], every[2 + shard, part, :])))
    width = COLUMNS * FEATS
    for layer in range(LAYERS):
        for i, part in enumerate(parts):
            send[layer, i * PART : (i + 1) * PART] = part
        send[layer, 64:96] = turned[layer * width : (layer + 1) * width]
        send[layer, 96:104] = label[...]


def relay_kernel(came, send):
    for layer in range(LAYERS):
        row = layer * BLOCK
        for q in range(2):
            for y in range(COLUMNS):
                peer = q * COLUMNS + y
                send[peer, row : row + 4 * PART] = came[layer, q * 4 * PART : (q + 1) * 4 * PART]
                send[peer, row + 4 * PART : row + BLOCK] = came[layer, 64 + y * FEATS : 64 + (y + 1) * FEATS]
    labels = jnp.concatenate([came[layer, 96:97] for layer in range(LAYERS)], axis=0)
    for peer in range(PEERS):
        send[peer, LAYERS * BLOCK :] = labels


def route_kernel(picks, nodes, bins, route):
    pick = picks[...]
    column = jnp.concatenate([pick[:, n : n + 1] for n in range(NODES)], axis=0)
    features = bins.shape[1]
    hot = (lax.broadcasted_iota(jnp.int32, (NODES * SHARD, features), 1) == (column // BINS)).astype(BF16)
    value = lax.dot_general(hot, bins[...].astype(BF16), LAST_DIMS, preferred_element_type=F32)
    right = (value > (column % BINS).astype(F32)).astype(jnp.int32)
    node = nodes[...]
    out = 2 * node
    for n in range(NODES):
        out = out + jnp.where(node == n, right[n * SHARD : (n + 1) * SHARD], 0)
    route[...] = out


def left_kernel(taken, own, away, left, *buffers):
    xl, core, quarter = (lax.axis_index(a) for a in ("xl", "core", "xh"))
    class_id = lax.broadcasted_iota(jnp.int32, (PART, HALF), 0) + quarter * PART
    ids = [(class_id + (2 * xl + shard) * SHARD).astype(F32) for shard in range(2)]
    bin_range = lax.broadcasted_iota(jnp.int32, (BINS, HALF), 0).astype(BF16)
    one, zero = jnp.ones((), BF16), jnp.zeros((), BF16)

    def build(source, paired, mask):
        for layer in range(LAYERS):
            lanes = slice(layer * HALF, (layer + 1) * HALF)
            base = layer * BLOCK
            label = jnp.broadcast_to(taken[source, LAYERS * BLOCK + layer : LAYERS * BLOCK + layer + 1], (PART, HALF))
            tiles = []
            for shard in range(2):
                prob = taken[source, base + shard * PART : base + (shard + 1) * PART]
                node = taken[source, base + (2 + shard) * PART : base + (3 + shard) * PART]
                target = (label == ids[shard]).astype(F32)
                for value in (prob - target, 2.0 * prob * (1.0 - prob)):
                    tiles += [jnp.where(node == float(n), value, 0.0) for n in range(NODES)]
            paired[:, lanes] = jnp.concatenate(tiles, axis=0).astype(BF16)
            for f in range(FEATS):
                row = taken[source, base + 4 * PART + f : base + 4 * PART + f + 1]
                row = jnp.broadcast_to(row, (BINS, HALF)).astype(BF16)
                mask[f * BINS : (f + 1) * BINS, lanes] = jnp.where(bin_range >= row, one, zero)

    def multiply(paired, mask):
        left[...] += lax.dot_general(mask[...], paired[...], LAST_DIMS, preferred_element_type=F32)

    even, odd = buffers[:2], buffers[2:]
    left[...] = jnp.zeros_like(left)
    build(0, *even)

    @pl.loop(0, PEERS // 2)
    def _(pair):
        build(2 * pair + 1, *odd)
        multiply(*even)
        build(jnp.minimum(2 * pair + 2, PEERS - 1), *even)
        multiply(*odd)

    middle = FEATS * BINS // 2
    low = lax.broadcasted_iota(jnp.int32, (BINS, 128), 1) < 64
    for row in range(0, middle, BINS):
        a, b = left[row : row + BINS], left[middle + row : middle + row + BINS]
        first = jnp.where(low, a, pltpu.roll(b, 64, 1))
        second = jnp.where(low, pltpu.roll(a, 64, 1), b)
        own[row : row + BINS] = jnp.where(core == 0, first, second)
        away[row : row + BINS] = jnp.where(core == 0, second, first)


def gain_kernel(target, own, other, spread):
    group = lax.axis_index("z") * COLUMNS + lax.axis_index("y")
    lane = lax.broadcasted_iota(jnp.int32, (1, 128), 1)
    pick = target[:1] - group * (FEATS * BINS) - jnp.where(lane >= 64, FEATS * BINS // 2, 0)
    line = lax.broadcasted_iota(jnp.int32, (BINS, 128), 0)
    best = jnp.full((BINS, 128), -jnp.inf, F32)
    sums = jnp.zeros((BINS, 128), F32)
    totals = jnp.zeros((1, 128), F32)
    for f in range(FEATS // 2):
        rows = slice(f * BINS, (f + 1) * BINS)
        g = own[rows] + other[rows]
        h = pltpu.roll(g, 96, 1)
        gt, ht = g[BINS - 1 :], h[BINS - 1 :]
        gain = 0.5 * (g * g / (h + reg_lambda) + (gt - g) ** 2 / (ht - h + reg_lambda) - gt * gt / (ht + reg_lambda))
        best = jnp.maximum(best, jnp.where(line == BINS - 1, -jnp.inf, gain))
        sums = jnp.where(line + f * BINS == pick, g, sums)
        inside = (pick >= f * BINS) & (pick < (f + 1) * BINS)
        totals = jnp.where(inside, gt, totals)
    best = jnp.max(best, axis=0, keepdims=True)
    sums = jnp.sum(sums, axis=0, keepdims=True)
    best = jnp.maximum(best, pltpu.roll(best, 64, 1))
    sums = sums + pltpu.roll(sums, 64, 1)
    totals = totals + pltpu.roll(totals, 64, 1)
    block = jnp.concatenate([best, jnp.where(lane < 64, sums, totals)], axis=0)
    for chip in range(spread.shape[0]):
        spread[chip] = block


def finish_kernel(gathered, scores, route, best, new_scores):
    chips = gathered.shape[0]
    weights = []
    for q in range(2):
        blocks = [gathered[chip] for chip in range(q * chips // 2, (q + 1) * chips // 2)]
        top, total = blocks[0], blocks[0]
        for block in blocks[1:]:
            top = jnp.maximum(top, block)
            total = total + block
        for n in range(NODES):
            best[n : n + 1, q * PART : (q + 1) * PART] = top[0:1, n * PART : (n + 1) * PART]
        total = total[1:2]
        gl = total
        hl, gt, ht = (pltpu.roll(total, 128 - 32 * j, 1) for j in (1, 2, 3))
        weights.append(-gl / (hl + reg_lambda))
        weights.append(-(gt - gl) / (ht - hl + reg_lambda))
    columns = jnp.concatenate(weights + [jnp.zeros((4, 128), F32)], axis=0).T
    way = route[...]
    for q in range(2):
        part = slice(q * PART, (q + 1) * PART)
        leaf = jnp.zeros((PART, way.shape[1]), F32)
        for n in range(NODES):
            for side in range(2):
                value = columns[n * PART : (n + 1) * PART, 2 * q + side : 2 * q + side + 1]
                leaf = jnp.where(way[part] == 2 * n + side, value, leaf)
        new_scores[part] = scores[part] + learn_rate * leaf


def neighbours():
    return [
        [((first if xh == 0 else 1 - first) * 2 + xh) * COLUMNS + y for xh in range(2) for y in range(COLUMNS)]
        for first in range(2)
    ]


def per_device(scores, labels, nodes, bins, pick_feature, pick_bin):
    rows = 2 * HALF
    chips = PEERS * LAYERS
    scores_t, nodes_t = scores.T, nodes.T
    shape = lambda *s: jax.ShapeDtypeStruct(s, F32)

    inputs = [PIN(x) for x in (scores_t, nodes_t, labels[None], bins, pick_feature.T, pick_bin.T)]
    joined, turned, label, target = call(
        join_kernel, "join",
        (
            shape(2 * SHARD, rows), shape(bins.shape[1], HALF), shape(8, HALF),
            jax.ShapeDtypeStruct((8, 128), jnp.int32),
        ),
        [HBM] * 6, inputs,
        scratch=[
            pltpu.VMEM((SHARD, rows), jnp.int32),
            pltpu.VMEM((1, rows), jnp.int32),
            pltpu.VMEM((HALF, bins.shape[1]), jnp.int32),
            pltpu.SMEM((2, NODES, SHARD), jnp.int32),
            pltpu.SemaphoreType.DMA((6,)),
        ],
    )
    every = lax.all_gather(joined, CLS)
    send = call(prepare_kernel, "prepare", shape(LAYERS, 104, HALF), [VMEM] * 3, (every, turned, label))
    came = lax.all_to_all(send, "z", 0, 0)
    send = call(relay_kernel, "relay", shape(PEERS, LAYERS * (BLOCK + 1), HALF), [VMEM], (came,))
    taken = lax.all_to_all(send, ("xl", "xh", "y"), 0, 0, axis_index_groups=neighbours())
    buffer = [pltpu.VMEM((128, LAYERS * HALF), BF16), pltpu.VMEM((FEATS * BINS, LAYERS * HALF), BF16)]
    half = shape(FEATS * BINS // 2, 128)
    own, away = call(
        left_kernel, "left", (half, half), [VMEM], (taken,),
        scratch=[pltpu.VMEM((FEATS * BINS, 128), F32)] + buffer + buffer, mib=32,
    )
    other = lax.ppermute(away, "core", [(0, 1), (1, 0)])
    pick_feature, pick_bin, own = lax.optimization_barrier((pick_feature, pick_bin, own))
    picks = pick_feature * BINS + pick_bin
    route = call(
        route_kernel, "route", jax.ShapeDtypeStruct((SHARD, rows), jnp.int32), [VMEM] * 3, (picks, nodes_t, bins)
    )
    other, route = lax.optimization_barrier((other, route))
    spread = call(gain_kernel, "gain", shape(chips, 2, 128), [VMEM] * 3, (target, own, other))
    gathered = lax.all_to_all(spread, ROW, 0, 0)
    best, new_scores = call(
        finish_kernel, "finish", (shape(NODES, SHARD), shape(SHARD, rows)), [VMEM] * 3, (gathered, scores_t, route)
    )
    return best.T, new_scores.T


def solution(mesh):
    fine = Mesh(mesh.devices.reshape(2, 2, 2, LAYERS, COLUMNS), CLS + ROW)
    in_specs = (P(ROW, CLS), P(ROW), P(ROW, CLS), P(ROW, None), P(CLS, None), P(CLS, None))
    out_specs = (P(CLS, None), P(ROW, CLS))
    return jax.shard_map(per_device, mesh=fine, in_specs=in_specs, out_specs=out_specs, check_vma=False)
```

```python
import jax
import jax.numpy as jnp
from jax import lax
from jax.experimental import pallas as pl
from jax.experimental.pallas import tpu as pltpu
from jax.sharding import Mesh, PartitionSpec as P

BINS = 128
NODES = 4
SHARD = 16
HALF = 128
PART = 8
FEATS = 8
LAYERS = 8
COLUMNS = 4
BLOCK = 4 * PART + FEATS
PEERS = 2 * COLUMNS

reg_lambda = 1.0
learn_rate = 0.5

CLS = ("xl", "core")
ROW = ("xh", "z", "y")
VMEM = pl.BlockSpec(memory_space=pltpu.VMEM)
HBM = pl.BlockSpec(memory_space=pltpu.HBM)
SMEM = pl.BlockSpec(memory_space=pltpu.SMEM)
BF16 = jnp.bfloat16
F32 = jnp.float32
PIN = lambda x: pltpu.with_memory_space_constraint(x, pltpu.HBM)
LAST_DIMS = (((1,), (1,)), ((), ()))


def params(mib):
    return pltpu.CompilerParams(vmem_limit_bytes=mib * 1024 * 1024)


def call(kernel, name, shapes, specs, args, scratch=(), mib=16):
    many = isinstance(shapes, tuple)
    return pl.pallas_call(
        kernel,
        out_shape=shapes,
        in_specs=specs,
        out_specs=(VMEM,) * len(shapes) if many else VMEM,
        scratch_shapes=list(scratch),
        compiler_params=params(mib),
        name=name,
    )(*args)


def join_kernel(
    scores, nodes, labels, bins, pick_feature, pick_bin, joined, turned, label, target,
    node_buffer, label_buffer, columns, picked, sems,
):
    core, quarter = lax.axis_index("core"), lax.axis_index("xh")
    start = pl.multiple_of(core * HALF, HALF)
    copies = [
        pltpu.make_async_copy(bins.at[pl.ds(start, HALF), :], columns, sems.at[0]),
        pltpu.make_async_copy(scores, joined.at[pl.ds(0, SHARD), :], sems.at[1]),
        pltpu.make_async_copy(nodes, node_buffer, sems.at[2]),
        pltpu.make_async_copy(labels, label_buffer, sems.at[3]),
        pltpu.make_async_copy(pick_feature, picked.at[0], sems.at[4]),
        pltpu.make_async_copy(pick_bin, picked.at[1], sems.at[5]),
    ]
    for copy in copies:
        copy.start()
    for copy in copies:
        copy.wait()
    joined[SHARD:] = node_buffer[...].astype(F32)
    turned[...] = columns[...].astype(F32).T
    row = label_buffer[...].astype(F32)
    label[...] = jnp.broadcast_to(jnp.where(core == 0, row[:, :HALF], row[:, HALF:]), label.shape)
    lane = lax.broadcasted_iota(jnp.int32, target.shape, 1) % (NODES * PART)
    chosen = jnp.zeros(target.shape, jnp.int32)
    for n in range(NODES):
        for k in range(PART):
            where = quarter * PART + k
            chosen = jnp.where(lane == n * PART + k, picked[0, n, where] * BINS + picked[1, n, where], chosen)
    target[...] = chosen


def prepare_kernel(every, turned, label, send):
    xl, core, xh = (lax.axis_index(a) for a in ("xl", "core", "xh"))

    def half(x):
        return jnp.where(core == 0, x[..., :HALF], x[..., HALF:])

    scores = [half(every[i, :SHARD, :]) for i in range(4)]
    top = jnp.max(jnp.maximum(jnp.maximum(scores[0], scores[1]), jnp.maximum(scores[2], scores[3])), axis=0, keepdims=True)
    exponent = [jnp.exp(s - top) for s in scores]
    denominator = jnp.sum((exponent[0] + exponent[1]) + (exponent[2] + exponent[3]), axis=0, keepdims=True)
    parts = []
    for q in range(2):
        low = (xl == 0) == (xh == q)
        part = slice(q * PART, (q + 1) * PART)
        for shard in range(2):
            parts.append(jnp.where(low, exponent[shard][part], exponent[2 + shard][part]) / denominator)
        part = slice(SHARD + q * PART, SHARD + (q + 1) * PART)
        for shard in range(2):
            parts.append(half(jnp.where(low, every[shard, part, :], every[2 + shard, part, :])))
    width = COLUMNS * FEATS
    for layer in range(LAYERS):
        for i, part in enumerate(parts):
            send[layer, i * PART : (i + 1) * PART] = part
        send[layer, 64:96] = turned[layer * width : (layer + 1) * width]
        send[layer, 96:104] = label[...]


def relay_kernel(came, send):
    for layer in range(LAYERS):
        row = layer * BLOCK
        for q in range(2):
            for y in range(COLUMNS):
                peer = q * COLUMNS + y
                send[peer, row : row + 4 * PART] = came[layer, q * 4 * PART : (q + 1) * 4 * PART]
                send[peer, row + 4 * PART : row + BLOCK] = came[layer, 64 + y * FEATS : 64 + (y + 1) * FEATS]
    labels = jnp.concatenate([came[layer, 96:97] for layer in range(LAYERS)], axis=0)
    for peer in range(PEERS):
        send[peer, LAYERS * BLOCK :] = labels


def route_kernel(picks, nodes, bins, route):
    pick = picks[...]
    column = jnp.concatenate([pick[:, n : n + 1] for n in range(NODES)], axis=0)
    features = bins.shape[1]
    hot = (lax.broadcasted_iota(jnp.int32, (NODES * SHARD, features), 1) == (column // BINS)).astype(BF16)
    value = lax.dot_general(hot, bins[...].astype(BF16), LAST_DIMS, preferred_element_type=F32)
    right = (value > (column % BINS).astype(F32)).astype(jnp.int32)
    node = nodes[...]
    out = 2 * node
    for n in range(NODES):
        out = out + jnp.where(node == n, right[n * SHARD : (n + 1) * SHARD], 0)
    route[...] = out


TURNED = 6


def left_kernel(taken, own, away, left, wide, *buffers):
    xl, core, quarter = (lax.axis_index(a) for a in ("xl", "core", "xh"))
    class_id = lax.broadcasted_iota(jnp.int32, (PART, HALF), 0) + quarter * PART
    ids = [(class_id + (2 * xl + shard) * SHARD).astype(F32) for shard in range(2)]
    bin_range = lax.broadcasted_iota(jnp.int32, (BINS, HALF), 0).astype(BF16)
    one, zero = jnp.ones((), BF16), jnp.zeros((), BF16)

    def build(source, paired, mask, turned):
        for layer in range(LAYERS):
            lanes = slice(layer * HALF, (layer + 1) * HALF)
            base = layer * BLOCK
            label = jnp.broadcast_to(taken[source, LAYERS * BLOCK + layer : LAYERS * BLOCK + layer + 1], (PART, HALF))
            tiles = []
            for shard in range(2):
                prob = taken[source, base + shard * PART : base + (shard + 1) * PART]
                node = taken[source, base + (2 + shard) * PART : base + (3 + shard) * PART]
                target = (label == ids[shard]).astype(F32)
                for value in (prob - target, 2.0 * prob * (1.0 - prob)):
                    tiles += [jnp.where(node == float(n), value, 0.0) for n in range(NODES)]
            paired[:, lanes] = jnp.concatenate(tiles, axis=0).astype(BF16)
            masks = []
            for f in range(FEATS):
                row = taken[source, base + 4 * PART + f : base + 4 * PART + f + 1]
                row = jnp.broadcast_to(row, (BINS, HALF)).astype(BF16)
                masks.append(jnp.where(bin_range >= row, one, zero))
            turned[lanes, :] = jnp.concatenate(masks[:TURNED], axis=0).T
            for i, tile in enumerate(masks[TURNED:]):
                mask[i * BINS : (i + 1) * BINS, lanes] = tile

    def multiply(paired, mask, turned):
        wide[...] += jnp.dot(paired[...], turned[...], preferred_element_type=F32)
        left[TURNED * BINS :] += lax.dot_general(mask[...], paired[...], LAST_DIMS, preferred_element_type=F32)

    even, odd = buffers[:3], buffers[3:]
    left[...] = jnp.zeros_like(left)
    wide[...] = jnp.zeros_like(wide)
    build(0, *even)

    @pl.loop(0, PEERS // 2)
    def _(pair):
        build(2 * pair + 1, *odd)
        multiply(*even)
        build(jnp.minimum(2 * pair + 2, PEERS - 1), *even)
        multiply(*odd)

    for f in range(TURNED):
        left[f * BINS : (f + 1) * BINS] = wide[:, f * BINS : (f + 1) * BINS].T
    middle = FEATS * BINS // 2
    low = lax.broadcasted_iota(jnp.int32, (BINS, 128), 1) < 64
    for row in range(0, middle, BINS):
        a, b = left[row : row + BINS], left[middle + row : middle + row + BINS]
        first = jnp.where(low, a, pltpu.roll(b, 64, 1))
        second = jnp.where(low, pltpu.roll(a, 64, 1), b)
        own[row : row + BINS] = jnp.where(core == 0, first, second)
        away[row : row + BINS] = jnp.where(core == 0, second, first)


def gain_kernel(target, own, other, spread):
    group = lax.axis_index("z") * COLUMNS + lax.axis_index("y")
    lane = lax.broadcasted_iota(jnp.int32, (1, 128), 1)
    pick = target[:1] - group * (FEATS * BINS) - jnp.where(lane >= 64, FEATS * BINS // 2, 0)
    line = lax.broadcasted_iota(jnp.int32, (BINS, 128), 0)
    best = jnp.full((BINS, 128), -jnp.inf, F32)
    sums = jnp.zeros((BINS, 128), F32)
    totals = jnp.zeros((1, 128), F32)
    for f in range(FEATS // 2):
        rows = slice(f * BINS, (f + 1) * BINS)
        g = own[rows] + other[rows]
        h = pltpu.roll(g, 96, 1)
        gt, ht = g[BINS - 1 :], h[BINS - 1 :]
        gain = 0.5 * (g * g / (h + reg_lambda) + (gt - g) ** 2 / (ht - h + reg_lambda) - gt * gt / (ht + reg_lambda))
        best = jnp.maximum(best, jnp.where(line == BINS - 1, -jnp.inf, gain))
        sums = jnp.where(line + f * BINS == pick, g, sums)
        inside = (pick >= f * BINS) & (pick < (f + 1) * BINS)
        totals = jnp.where(inside, gt, totals)
    best = jnp.max(best, axis=0, keepdims=True)
    sums = jnp.sum(sums, axis=0, keepdims=True)
    best = jnp.maximum(best, pltpu.roll(best, 64, 1))
    sums = sums + pltpu.roll(sums, 64, 1)
    totals = totals + pltpu.roll(totals, 64, 1)
    block = jnp.concatenate([best, jnp.where(lane < 64, sums, totals)], axis=0)
    for chip in range(spread.shape[0]):
        spread[chip] = block


def finish_kernel(gathered, scores, route, best, new_scores):
    chips = gathered.shape[0]
    weights = []
    for q in range(2):
        blocks = [gathered[chip] for chip in range(q * chips // 2, (q + 1) * chips // 2)]
        top, total = blocks[0], blocks[0]
        for block in blocks[1:]:
            top = jnp.maximum(top, block)
            total = total + block
        for n in range(NODES):
            best[n : n + 1, q * PART : (q + 1) * PART] = top[0:1, n * PART : (n + 1) * PART]
        total = total[1:2]
        gl = total
        hl, gt, ht = (pltpu.roll(total, 128 - 32 * j, 1) for j in (1, 2, 3))
        weights.append(-gl / (hl + reg_lambda))
        weights.append(-(gt - gl) / (ht - hl + reg_lambda))
    columns = jnp.concatenate(weights + [jnp.zeros((4, 128), F32)], axis=0).T
    way = route[...]
    for q in range(2):
        part = slice(q * PART, (q + 1) * PART)
        leaf = jnp.zeros((PART, way.shape[1]), F32)
        for n in range(NODES):
            for side in range(2):
                value = columns[n * PART : (n + 1) * PART, 2 * q + side : 2 * q + side + 1]
                leaf = jnp.where(way[part] == 2 * n + side, value, leaf)
        new_scores[part] = scores[part] + learn_rate * leaf


def neighbours():
    return [
        [((first if xh == 0 else 1 - first) * 2 + xh) * COLUMNS + y for xh in range(2) for y in range(COLUMNS)]
        for first in range(2)
    ]


def per_device(scores, labels, nodes, bins, pick_feature, pick_bin):
    rows = 2 * HALF
    chips = PEERS * LAYERS
    scores_t, nodes_t = scores.T, nodes.T
    shape = lambda *s: jax.ShapeDtypeStruct(s, F32)

    inputs = [PIN(x) for x in (scores_t, nodes_t, labels[None], bins, pick_feature.T, pick_bin.T)]
    joined, turned, label, target = call(
        join_kernel, "join",
        (
            shape(2 * SHARD, rows), shape(bins.shape[1], HALF), shape(8, HALF),
            jax.ShapeDtypeStruct((8, 128), jnp.int32),
        ),
        [HBM] * 6, inputs,
        scratch=[
            pltpu.VMEM((SHARD, rows), jnp.int32),
            pltpu.VMEM((1, rows), jnp.int32),
            pltpu.VMEM((HALF, bins.shape[1]), jnp.int32),
            pltpu.SMEM((2, NODES, SHARD), jnp.int32),
            pltpu.SemaphoreType.DMA((6,)),
        ],
    )
    every = lax.all_gather(joined, CLS)
    send = call(prepare_kernel, "prepare", shape(LAYERS, 104, HALF), [VMEM] * 3, (every, turned, label))
    came = lax.all_to_all(send, "z", 0, 0)
    send = call(relay_kernel, "relay", shape(PEERS, LAYERS * (BLOCK + 1), HALF), [VMEM], (came,))
    taken = lax.all_to_all(send, ("xl", "xh", "y"), 0, 0, axis_index_groups=neighbours())
    depth = LAYERS * HALF
    buffer = [
        pltpu.VMEM((128, depth), BF16),
        pltpu.VMEM(((FEATS - TURNED) * BINS, depth), BF16),
        pltpu.VMEM((depth, TURNED * BINS), BF16),
    ]
    half = shape(FEATS * BINS // 2, 128)
    own, away = call(
        left_kernel, "left", (half, half), [VMEM], (taken,),
        scratch=[pltpu.VMEM((FEATS * BINS, 128), F32), pltpu.VMEM((128, TURNED * BINS), F32)] + buffer + buffer, mib=32,
    )
    other = lax.ppermute(away, "core", [(0, 1), (1, 0)])
    pick_feature, pick_bin, own = lax.optimization_barrier((pick_feature, pick_bin, own))
    picks = pick_feature * BINS + pick_bin
    route = call(
        route_kernel, "route", jax.ShapeDtypeStruct((SHARD, rows), jnp.int32), [VMEM] * 3, (picks, nodes_t, bins)
    )
    other, route = lax.optimization_barrier((other, route))
    spread = call(gain_kernel, "gain", shape(chips, 2, 128), [VMEM] * 3, (target, own, other))
    gathered = lax.all_to_all(spread, ROW, 0, 0)
    best, new_scores = call(
        finish_kernel, "finish", (shape(NODES, SHARD), shape(SHARD, rows)), [VMEM] * 3, (gathered, scores_t, route)
    )
    return best.T, new_scores.T


def solution(mesh):
    fine = Mesh(mesh.devices.reshape(2, 2, 2, LAYERS, COLUMNS), CLS + ROW)
    in_specs = (P(ROW, CLS), P(ROW), P(ROW, CLS), P(ROW, None), P(CLS, None), P(CLS, None))
    out_specs = (P(CLS, None), P(ROW, CLS))
    return jax.shard_map(per_device, mesh=fine, in_specs=in_specs, out_specs=out_specs, check_vma=False)
```

```python
import jax
import jax.numpy as jnp
from jax import lax
from jax.experimental import pallas as pl
from jax.experimental.pallas import tpu as pltpu
from jax.sharding import Mesh, PartitionSpec as P

BINS = 128
NODES = 4
SHARD = 16
HALF = 128
PART = 8
FEATS = 8
LAYERS = 8
COLUMNS = 4
BLOCK = 4 * PART + FEATS
PEERS = 2 * COLUMNS

reg_lambda = 1.0
learn_rate = 0.5

CLS = ("xl", "core")
ROW = ("xh", "z", "y")
VMEM = pl.BlockSpec(memory_space=pltpu.VMEM)
HBM = pl.BlockSpec(memory_space=pltpu.HBM)
SMEM = pl.BlockSpec(memory_space=pltpu.SMEM)
BF16 = jnp.bfloat16
F32 = jnp.float32
PIN = lambda x: pltpu.with_memory_space_constraint(x, pltpu.HBM)
LAST_DIMS = (((1,), (1,)), ((), ()))


def params(mib):
    return pltpu.CompilerParams(vmem_limit_bytes=mib * 1024 * 1024)


def call(kernel, name, shapes, specs, args, scratch=(), mib=16):
    many = isinstance(shapes, tuple)
    return pl.pallas_call(
        kernel,
        out_shape=shapes,
        in_specs=specs,
        out_specs=(VMEM,) * len(shapes) if many else VMEM,
        scratch_shapes=list(scratch),
        compiler_params=params(mib),
        name=name,
    )(*args)


def join_kernel(
    scores, nodes, labels, bins, pick_feature, pick_bin, joined, turned, label, target,
    node_buffer, label_buffer, columns, picked, sems,
):
    core, quarter = lax.axis_index("core"), lax.axis_index("xh")
    start = pl.multiple_of(core * HALF, HALF)
    copies = [
        pltpu.make_async_copy(bins.at[pl.ds(start, HALF), :], columns, sems.at[0]),
        pltpu.make_async_copy(scores, joined.at[pl.ds(0, SHARD), :], sems.at[1]),
        pltpu.make_async_copy(nodes, node_buffer, sems.at[2]),
        pltpu.make_async_copy(labels, label_buffer, sems.at[3]),
        pltpu.make_async_copy(pick_feature, picked.at[0], sems.at[4]),
        pltpu.make_async_copy(pick_bin, picked.at[1], sems.at[5]),
    ]
    for copy in copies:
        copy.start()
    for copy in copies:
        copy.wait()
    joined[SHARD:] = node_buffer[...].astype(F32)
    turned[...] = columns[...].astype(F32).T
    row = label_buffer[...].astype(F32)
    label[...] = jnp.broadcast_to(jnp.where(core == 0, row[:, :HALF], row[:, HALF:]), label.shape)
    lane = lax.broadcasted_iota(jnp.int32, target.shape, 1) % (NODES * PART)
    chosen = jnp.zeros(target.shape, jnp.int32)
    for n in range(NODES):
        for k in range(PART):
            where = quarter * PART + k
            chosen = jnp.where(lane == n * PART + k, picked[0, n, where] * BINS + picked[1, n, where], chosen)
    target[...] = chosen


def prepare_kernel(every, turned, label, send):
    xl, core, xh = (lax.axis_index(a) for a in ("xl", "core", "xh"))

    def half(x):
        return jnp.where(core == 0, x[..., :HALF], x[..., HALF:])

    scores = [half(every[i, :SHARD, :]) for i in range(4)]
    top = jnp.max(jnp.maximum(jnp.maximum(scores[0], scores[1]), jnp.maximum(scores[2], scores[3])), axis=0, keepdims=True)
    exponent = [jnp.exp(s - top) for s in scores]
    denominator = jnp.sum((exponent[0] + exponent[1]) + (exponent[2] + exponent[3]), axis=0, keepdims=True)
    parts = []
    for q in range(2):
        low = (xl == 0) == (xh == q)
        part = slice(q * PART, (q + 1) * PART)
        for shard in range(2):
            parts.append(jnp.where(low, exponent[shard][part], exponent[2 + shard][part]) / denominator)
        part = slice(SHARD + q * PART, SHARD + (q + 1) * PART)
        for shard in range(2):
            parts.append(half(jnp.where(low, every[shard, part, :], every[2 + shard, part, :])))
    width = COLUMNS * FEATS
    for layer in range(LAYERS):
        for i, part in enumerate(parts):
            send[layer, i * PART : (i + 1) * PART] = part
        send[layer, 64:96] = turned[layer * width : (layer + 1) * width]
        send[layer, 96:104] = label[...]


def relay_kernel(came, send):
    for layer in range(LAYERS):
        row = layer * BLOCK
        for q in range(2):
            for y in range(COLUMNS):
                peer = q * COLUMNS + y
                send[peer, row : row + 4 * PART] = came[layer, q * 4 * PART : (q + 1) * 4 * PART]
                send[peer, row + 4 * PART : row + BLOCK] = came[layer, 64 + y * FEATS : 64 + (y + 1) * FEATS]
    labels = jnp.concatenate([came[layer, 96:97] for layer in range(LAYERS)], axis=0)
    for peer in range(PEERS):
        send[peer, LAYERS * BLOCK :] = labels


def route_kernel(picks, nodes, bins, route):
    pick = picks[...]
    column = jnp.concatenate([pick[:, n : n + 1] for n in range(NODES)], axis=0)
    features = bins.shape[1]
    hot = (lax.broadcasted_iota(jnp.int32, (NODES * SHARD, features), 1) == (column // BINS)).astype(BF16)
    value = lax.dot_general(hot, bins[...].astype(BF16), LAST_DIMS, preferred_element_type=F32)
    right = (value > (column % BINS).astype(F32)).astype(jnp.int32)
    node = nodes[...]
    out = 2 * node
    for n in range(NODES):
        out = out + jnp.where(node == n, right[n * SHARD : (n + 1) * SHARD], 0)
    route[...] = out


TURNED = (0, 1, 2, 4, 5, 6)
STREAMED = (3, 7)


def left_kernel(taken, own, away, left, wide, *buffers):
    xl, core, quarter = (lax.axis_index(a) for a in ("xl", "core", "xh"))
    class_id = lax.broadcasted_iota(jnp.int32, (PART, HALF), 0) + quarter * PART
    ids = [(class_id + (2 * xl + shard) * SHARD).astype(F32) for shard in range(2)]
    bin_range = lax.broadcasted_iota(jnp.int32, (BINS, HALF), 0).astype(BF16)
    one, zero = jnp.ones((), BF16), jnp.zeros((), BF16)

    def build(source, paired, mask, turned):
        for layer in range(LAYERS):
            lanes = slice(layer * HALF, (layer + 1) * HALF)
            base = layer * BLOCK
            label = jnp.broadcast_to(taken[source, LAYERS * BLOCK + layer : LAYERS * BLOCK + layer + 1], (PART, HALF))
            tiles = []
            for shard in range(2):
                prob = taken[source, base + shard * PART : base + (shard + 1) * PART]
                node = taken[source, base + (2 + shard) * PART : base + (3 + shard) * PART]
                target = (label == ids[shard]).astype(F32)
                for value in (prob - target, 2.0 * prob * (1.0 - prob)):
                    tiles += [jnp.where(node == float(n), value, 0.0) for n in range(NODES)]
            paired[:, lanes] = jnp.concatenate(tiles, axis=0).astype(BF16)
            masks = []
            for f in range(FEATS):
                row = taken[source, base + 4 * PART + f : base + 4 * PART + f + 1]
                row = jnp.broadcast_to(row, (BINS, HALF)).astype(BF16)
                masks.append(jnp.where(bin_range >= row, one, zero))
            turned[lanes, :] = jnp.concatenate([masks[f] for f in TURNED], axis=0).T
            for i, f in enumerate(STREAMED):
                mask[i * BINS : (i + 1) * BINS, lanes] = masks[f]

    def multiply(paired, mask, turned):
        wide[...] += jnp.dot(paired[...], turned[...], preferred_element_type=F32)
        left[...] += lax.dot_general(mask[...], paired[...], LAST_DIMS, preferred_element_type=F32)

    even, odd = buffers[:3], buffers[3:]
    left[...] = jnp.zeros_like(left)
    wide[...] = jnp.zeros_like(wide)
    build(0, *even)

    @pl.loop(0, PEERS // 2 - 1)
    def _(pair):
        build(2 * pair + 1, *odd)
        multiply(*even)
        build(2 * pair + 2, *even)
        multiply(*odd)

    build(PEERS - 1, *odd)
    multiply(*even)
    multiply(*odd)

    for out, shard in ((own, core), (away, 1 - core)):
        rows = pl.ds(pl.multiple_of(shard * 64, 64), 64)
        for i, f in enumerate(TURNED[: len(TURNED) // 2]):
            j = i + len(TURNED) // 2
            tiles = [wide[rows, k * BINS : (k + 1) * BINS] for k in (i, j)]
            out[f * BINS : (f + 1) * BINS] = jnp.concatenate(tiles, axis=0).T
    low = lax.broadcasted_iota(jnp.int32, (BINS, 128), 1) < 64
    a, b = left[:BINS], left[BINS:]
    first = jnp.where(low, a, pltpu.roll(b, 64, 1))
    second = jnp.where(low, pltpu.roll(a, 64, 1), b)
    f = STREAMED[0]
    own[f * BINS : (f + 1) * BINS] = jnp.where(core == 0, first, second)
    away[f * BINS : (f + 1) * BINS] = jnp.where(core == 0, second, first)


def gain_kernel(target, own, other, spread):
    group = lax.axis_index("z") * COLUMNS + lax.axis_index("y")
    lane = lax.broadcasted_iota(jnp.int32, (1, 128), 1)
    pick = target[:1] - group * (FEATS * BINS) - jnp.where(lane >= 64, FEATS * BINS // 2, 0)
    line = lax.broadcasted_iota(jnp.int32, (BINS, 128), 0)
    best = jnp.full((BINS, 128), -jnp.inf, F32)
    sums = jnp.zeros((BINS, 128), F32)
    totals = jnp.zeros((1, 128), F32)
    for f in range(FEATS // 2):
        rows = slice(f * BINS, (f + 1) * BINS)
        g = own[rows] + other[rows]
        h = pltpu.roll(g, 96, 1)
        gt, ht = g[BINS - 1 :], h[BINS - 1 :]
        gain = 0.5 * (g * g / (h + reg_lambda) + (gt - g) ** 2 / (ht - h + reg_lambda) - gt * gt / (ht + reg_lambda))
        best = jnp.maximum(best, jnp.where(line == BINS - 1, -jnp.inf, gain))
        sums = jnp.where(line + f * BINS == pick, g, sums)
        inside = (pick >= f * BINS) & (pick < (f + 1) * BINS)
        totals = jnp.where(inside, gt, totals)
    best = jnp.max(best, axis=0, keepdims=True)
    sums = jnp.sum(sums, axis=0, keepdims=True)
    best = jnp.maximum(best, pltpu.roll(best, 64, 1))
    sums = sums + pltpu.roll(sums, 64, 1)
    totals = totals + pltpu.roll(totals, 64, 1)
    block = jnp.concatenate([best, jnp.where(lane < 64, sums, totals)], axis=0)
    for chip in range(spread.shape[0]):
        spread[chip] = block


def finish_kernel(gathered, scores, route, best, new_scores):
    chips = gathered.shape[0]
    weights = []
    for q in range(2):
        blocks = [gathered[chip] for chip in range(q * chips // 2, (q + 1) * chips // 2)]
        top, total = blocks[0], blocks[0]
        for block in blocks[1:]:
            top = jnp.maximum(top, block)
            total = total + block
        for n in range(NODES):
            best[n : n + 1, q * PART : (q + 1) * PART] = top[0:1, n * PART : (n + 1) * PART]
        total = total[1:2]
        gl = total
        hl, gt, ht = (pltpu.roll(total, 128 - 32 * j, 1) for j in (1, 2, 3))
        weights.append(-gl / (hl + reg_lambda))
        weights.append(-(gt - gl) / (ht - hl + reg_lambda))
    columns = jnp.concatenate(weights + [jnp.zeros((4, 128), F32)], axis=0).T
    way = route[...]
    for q in range(2):
        part = slice(q * PART, (q + 1) * PART)
        leaf = jnp.zeros((PART, way.shape[1]), F32)
        for n in range(NODES):
            for side in range(2):
                value = columns[n * PART : (n + 1) * PART, 2 * q + side : 2 * q + side + 1]
                leaf = jnp.where(way[part] == 2 * n + side, value, leaf)
        new_scores[part] = scores[part] + learn_rate * leaf


def neighbours():
    return [
        [((first if xh == 0 else 1 - first) * 2 + xh) * COLUMNS + y for xh in range(2) for y in range(COLUMNS)]
        for first in range(2)
    ]


def per_device(scores, labels, nodes, bins, pick_feature, pick_bin):
    rows = 2 * HALF
    chips = PEERS * LAYERS
    scores_t, nodes_t = scores.T, nodes.T
    shape = lambda *s: jax.ShapeDtypeStruct(s, F32)

    inputs = [PIN(x) for x in (scores_t, nodes_t, labels[None], bins, pick_feature.T, pick_bin.T)]
    joined, turned, label, target = call(
        join_kernel, "join",
        (
            shape(2 * SHARD, rows), shape(bins.shape[1], HALF), shape(8, HALF),
            jax.ShapeDtypeStruct((8, 128), jnp.int32),
        ),
        [HBM] * 6, inputs,
        scratch=[
            pltpu.VMEM((SHARD, rows), jnp.int32),
            pltpu.VMEM((1, rows), jnp.int32),
            pltpu.VMEM((HALF, bins.shape[1]), jnp.int32),
            pltpu.SMEM((2, NODES, SHARD), jnp.int32),
            pltpu.SemaphoreType.DMA((6,)),
        ],
    )
    every = lax.all_gather(joined, CLS)
    send = call(prepare_kernel, "prepare", shape(LAYERS, 104, HALF), [VMEM] * 3, (every, turned, label))
    came = lax.all_to_all(send, "z", 0, 0)
    send = call(relay_kernel, "relay", shape(PEERS, LAYERS * (BLOCK + 1), HALF), [VMEM], (came,))
    taken = lax.all_to_all(send, ("xl", "xh", "y"), 0, 0, axis_index_groups=neighbours())
    depth = LAYERS * HALF
    buffer = [
        pltpu.VMEM((128, depth), BF16),
        pltpu.VMEM((len(STREAMED) * BINS, depth), BF16),
        pltpu.VMEM((depth, len(TURNED) * BINS), BF16),
    ]
    half = shape(FEATS * BINS // 2, 128)
    own, away = call(
        left_kernel, "left", (half, half), [VMEM], (taken,),
        scratch=[pltpu.VMEM((len(STREAMED) * BINS, 128), F32), pltpu.VMEM((128, len(TURNED) * BINS), F32)] + buffer + buffer, mib=32,
    )
    other = lax.ppermute(away, "core", [(0, 1), (1, 0)])
    pick_feature, pick_bin, own = lax.optimization_barrier((pick_feature, pick_bin, own))
    picks = pick_feature * BINS + pick_bin
    route = call(
        route_kernel, "route", jax.ShapeDtypeStruct((SHARD, rows), jnp.int32), [VMEM] * 3, (picks, nodes_t, bins)
    )
    other, route = lax.optimization_barrier((other, route))
    spread = call(gain_kernel, "gain", shape(chips, 2, 128), [VMEM] * 3, (target, own, other))
    gathered = lax.all_to_all(spread, ROW, 0, 0)
    best, new_scores = call(
        finish_kernel, "finish", (shape(NODES, SHARD), shape(SHARD, rows)), [VMEM] * 3, (gathered, scores_t, route)
    )
    return best.T, new_scores.T


def solution(mesh):
    fine = Mesh(mesh.devices.reshape(2, 2, 2, LAYERS, COLUMNS), CLS + ROW)
    in_specs = (P(ROW, CLS), P(ROW), P(ROW, CLS), P(ROW, None), P(CLS, None), P(CLS, None))
    out_specs = (P(CLS, None), P(ROW, CLS))
    return jax.shard_map(per_device, mesh=fine, in_specs=in_specs, out_specs=out_specs, check_vma=False)
```

```python
import jax
import jax.numpy as jnp
from jax import lax
from jax.experimental import pallas as pl
from jax.experimental.pallas import tpu as pltpu
from jax.sharding import Mesh, PartitionSpec as P

BINS = 128
NODES = 4
SHARD = 16
HALF = 128
PART = 8
FEATS = 8
LAYERS = 8
COLUMNS = 4
BLOCK = 4 * PART + FEATS
PEERS = 2 * COLUMNS

reg_lambda = 1.0
learn_rate = 0.5

CLS = ("xl", "core")
ROW = ("xh", "z", "y")
VMEM = pl.BlockSpec(memory_space=pltpu.VMEM)
HBM = pl.BlockSpec(memory_space=pltpu.HBM)
SMEM = pl.BlockSpec(memory_space=pltpu.SMEM)
BF16 = jnp.bfloat16
F32 = jnp.float32
PIN = lambda x: pltpu.with_memory_space_constraint(x, pltpu.HBM)
LAST_DIMS = (((1,), (1,)), ((), ()))


def params(mib):
    return pltpu.CompilerParams(vmem_limit_bytes=mib * 1024 * 1024)


def call(kernel, name, shapes, specs, args, scratch=(), mib=16):
    many = isinstance(shapes, tuple)
    return pl.pallas_call(
        kernel,
        out_shape=shapes,
        in_specs=specs,
        out_specs=(VMEM,) * len(shapes) if many else VMEM,
        scratch_shapes=list(scratch),
        compiler_params=params(mib),
        name=name,
    )(*args)


def join_kernel(
    scores, nodes, labels, bins, pick_feature, pick_bin, joined, turned, label, target,
    node_buffer, label_buffer, columns, picked, sems,
):
    core, quarter = lax.axis_index("core"), lax.axis_index("xh")
    start = pl.multiple_of(core * HALF, HALF)
    copies = [
        pltpu.make_async_copy(bins.at[pl.ds(start, HALF), :], columns, sems.at[0]),
        pltpu.make_async_copy(scores, joined.at[pl.ds(0, SHARD), :], sems.at[1]),
        pltpu.make_async_copy(nodes, node_buffer, sems.at[2]),
        pltpu.make_async_copy(labels, label_buffer, sems.at[3]),
        pltpu.make_async_copy(pick_feature, picked.at[0], sems.at[4]),
        pltpu.make_async_copy(pick_bin, picked.at[1], sems.at[5]),
    ]
    for copy in copies:
        copy.start()
    for copy in copies:
        copy.wait()
    joined[SHARD:] = node_buffer[...].astype(F32)
    turned[...] = columns[...].astype(F32).T
    row = label_buffer[...].astype(F32)
    label[...] = jnp.broadcast_to(jnp.where(core == 0, row[:, :HALF], row[:, HALF:]), label.shape)
    lane = lax.broadcasted_iota(jnp.int32, target.shape, 1) % (NODES * PART)
    chosen = jnp.zeros(target.shape, jnp.int32)
    for n in range(NODES):
        for k in range(PART):
            where = quarter * PART + k
            chosen = jnp.where(lane == n * PART + k, picked[0, n, where] * BINS + picked[1, n, where], chosen)
    target[...] = chosen


def prepare_kernel(every, turned, label, send):
    xl, core, xh = (lax.axis_index(a) for a in ("xl", "core", "xh"))

    def half(x):
        return jnp.where(core == 0, x[..., :HALF], x[..., HALF:])

    scores = [half(every[i, :SHARD, :]) for i in range(4)]
    top = jnp.max(jnp.maximum(jnp.maximum(scores[0], scores[1]), jnp.maximum(scores[2], scores[3])), axis=0, keepdims=True)
    exponent = [jnp.exp(s - top) for s in scores]
    denominator = jnp.sum((exponent[0] + exponent[1]) + (exponent[2] + exponent[3]), axis=0, keepdims=True)
    parts = []
    for q in range(2):
        low = (xl == 0) == (xh == q)
        part = slice(q * PART, (q + 1) * PART)
        for shard in range(2):
            parts.append(jnp.where(low, exponent[shard][part], exponent[2 + shard][part]) / denominator)
        part = slice(SHARD + q * PART, SHARD + (q + 1) * PART)
        for shard in range(2):
            parts.append(half(jnp.where(low, every[shard, part, :], every[2 + shard, part, :])))
    width = COLUMNS * FEATS
    for layer in range(LAYERS):
        for i, part in enumerate(parts):
            send[layer, i * PART : (i + 1) * PART] = part
        send[layer, 64:96] = turned[layer * width : (layer + 1) * width]
        send[layer, 96:104] = label[...]


def relay_kernel(came, send):
    for layer in range(LAYERS):
        row = layer * BLOCK
        for q in range(2):
            for y in range(COLUMNS):
                peer = q * COLUMNS + y
                send[peer, row : row + 4 * PART] = came[layer, q * 4 * PART : (q + 1) * 4 * PART]
                send[peer, row + 4 * PART : row + BLOCK] = came[layer, 64 + y * FEATS : 64 + (y + 1) * FEATS]
    labels = jnp.concatenate([came[layer, 96:97] for layer in range(LAYERS)], axis=0)
    for peer in range(PEERS):
        send[peer, LAYERS * BLOCK :] = labels


def route_kernel(picks, nodes, bins, route):
    pick = picks[...]
    column = jnp.concatenate([pick[:, n : n + 1] for n in range(NODES)], axis=0)
    features = bins.shape[1]
    hot = (lax.broadcasted_iota(jnp.int32, (NODES * SHARD, features), 1) == (column // BINS)).astype(BF16)
    value = lax.dot_general(hot, bins[...].astype(BF16), LAST_DIMS, preferred_element_type=F32)
    right = (value > (column % BINS).astype(F32)).astype(jnp.int32)
    node = nodes[...]
    out = 2 * node
    for n in range(NODES):
        out = out + jnp.where(node == n, right[n * SHARD : (n + 1) * SHARD], 0)
    route[...] = out


TURNED = (0, 1, 2, 4, 5, 6)
STREAMED = (3, 7)


def left_kernel(taken, own, away, left, wide, *buffers):
    xl, core, quarter = (lax.axis_index(a) for a in ("xl", "core", "xh"))
    class_id = lax.broadcasted_iota(jnp.int32, (PART, HALF), 0) + quarter * PART
    ids = [(class_id + (2 * xl + shard) * SHARD).astype(F32) for shard in range(2)]
    bin_range = lax.broadcasted_iota(jnp.int32, (BINS, HALF), 0).astype(BF16)
    one, zero = jnp.ones((), BF16), jnp.zeros((), BF16)

    def build(source, paired, mask, turned):
        for layer in range(LAYERS):
            lanes = slice(layer * HALF, (layer + 1) * HALF)
            base = layer * BLOCK
            label = jnp.broadcast_to(taken[source, LAYERS * BLOCK + layer : LAYERS * BLOCK + layer + 1], (PART, HALF))
            tiles = []
            for shard in range(2):
                prob = taken[source, base + shard * PART : base + (shard + 1) * PART]
                node = taken[source, base + (2 + shard) * PART : base + (3 + shard) * PART]
                target = (label == ids[shard]).astype(F32)
                for value in (prob - target, 2.0 * prob * (1.0 - prob)):
                    tiles += [jnp.where(node == float(n), value, 0.0) for n in range(NODES)]
            paired[:, lanes] = jnp.concatenate(tiles, axis=0).astype(BF16)
            masks = []
            for f in range(FEATS):
                row = taken[source, base + 4 * PART + f : base + 4 * PART + f + 1]
                row = jnp.broadcast_to(row, (BINS, HALF)).astype(BF16)
                masks.append(jnp.where(bin_range >= row, one, zero))
            turned[lanes, :] = jnp.concatenate([masks[f] for f in TURNED], axis=0).T
            for i, f in enumerate(STREAMED):
                mask[i * BINS : (i + 1) * BINS, lanes] = masks[f]

    def multiply(paired, mask, turned):
        left[...] += lax.dot_general(mask[...], paired[...], LAST_DIMS, preferred_element_type=F32)
        wide[...] += jnp.dot(paired[...], turned[...], preferred_element_type=F32)

    even, odd = buffers[:3], buffers[3:]
    left[...] = jnp.zeros_like(left)
    wide[...] = jnp.zeros_like(wide)
    build(0, *even)

    @pl.loop(0, PEERS // 2 - 1)
    def _(pair):
        build(2 * pair + 1, *odd)
        multiply(*even)
        build(2 * pair + 2, *even)
        multiply(*odd)

    build(PEERS - 1, *odd)
    multiply(*even)
    multiply(*odd)

    for out, shard in ((own, core), (away, 1 - core)):
        rows = pl.ds(pl.multiple_of(shard * 64, 64), 64)
        for i, f in enumerate(TURNED[: len(TURNED) // 2]):
            j = i + len(TURNED) // 2
            tiles = [wide[rows, k * BINS : (k + 1) * BINS] for k in (i, j)]
            out[f * BINS : (f + 1) * BINS] = jnp.concatenate(tiles, axis=0).T
    low = lax.broadcasted_iota(jnp.int32, (BINS, 128), 1) < 64
    a, b = left[:BINS], left[BINS:]
    first = jnp.where(low, a, pltpu.roll(b, 64, 1))
    second = jnp.where(low, pltpu.roll(a, 64, 1), b)
    f = STREAMED[0]
    own[f * BINS : (f + 1) * BINS] = jnp.where(core == 0, first, second)
    away[f * BINS : (f + 1) * BINS] = jnp.where(core == 0, second, first)


def gain_kernel(target, own, other, spread):
    group = lax.axis_index("z") * COLUMNS + lax.axis_index("y")
    lane = lax.broadcasted_iota(jnp.int32, (1, 128), 1)
    pick = target[:1] - group * (FEATS * BINS) - jnp.where(lane >= 64, FEATS * BINS // 2, 0)
    line = lax.broadcasted_iota(jnp.int32, (BINS, 128), 0)
    best = jnp.full((BINS, 128), -jnp.inf, F32)
    sums = jnp.zeros((BINS, 128), F32)
    totals = jnp.zeros((1, 128), F32)
    for f in range(FEATS // 2):
        rows = slice(f * BINS, (f + 1) * BINS)
        g = own[rows] + other[rows]
        h = pltpu.roll(g, 96, 1)
        gt, ht = g[BINS - 1 :], h[BINS - 1 :]
        gain = 0.5 * (g * g / (h + reg_lambda) + (gt - g) ** 2 / (ht - h + reg_lambda) - gt * gt / (ht + reg_lambda))
        best = jnp.maximum(best, jnp.where(line == BINS - 1, -jnp.inf, gain))
        sums = jnp.where(line + f * BINS == pick, g, sums)
        inside = (pick >= f * BINS) & (pick < (f + 1) * BINS)
        totals = jnp.where(inside, gt, totals)
    best = jnp.max(best, axis=0, keepdims=True)
    sums = jnp.sum(sums, axis=0, keepdims=True)
    best = jnp.maximum(best, pltpu.roll(best, 64, 1))
    sums = sums + pltpu.roll(sums, 64, 1)
    totals = totals + pltpu.roll(totals, 64, 1)
    block = jnp.concatenate([best, jnp.where(lane < 64, sums, totals)], axis=0)
    for chip in range(spread.shape[0]):
        spread[chip] = block


def finish_kernel(gathered, scores, route, best, new_scores):
    chips = gathered.shape[0]
    weights = []
    for q in range(2):
        blocks = [gathered[chip] for chip in range(q * chips // 2, (q + 1) * chips // 2)]
        top, total = blocks[0], blocks[0]
        for block in blocks[1:]:
            top = jnp.maximum(top, block)
            total = total + block
        for n in range(NODES):
            best[n : n + 1, q * PART : (q + 1) * PART] = top[0:1, n * PART : (n + 1) * PART]
        total = total[1:2]
        gl = total
        hl, gt, ht = (pltpu.roll(total, 128 - 32 * j, 1) for j in (1, 2, 3))
        weights.append(-gl / (hl + reg_lambda))
        weights.append(-(gt - gl) / (ht - hl + reg_lambda))
    columns = jnp.concatenate(weights + [jnp.zeros((4, 128), F32)], axis=0).T
    way = route[...]
    for q in range(2):
        part = slice(q * PART, (q + 1) * PART)
        leaf = jnp.zeros((PART, way.shape[1]), F32)
        for n in range(NODES):
            for side in range(2):
                value = columns[n * PART : (n + 1) * PART, 2 * q + side : 2 * q + side + 1]
                leaf = jnp.where(way[part] == 2 * n + side, value, leaf)
        new_scores[part] = scores[part] + learn_rate * leaf


def neighbours():
    return [
        [((first if xh == 0 else 1 - first) * 2 + xh) * COLUMNS + y for xh in range(2) for y in range(COLUMNS)]
        for first in range(2)
    ]


def per_device(scores, labels, nodes, bins, pick_feature, pick_bin):
    rows = 2 * HALF
    chips = PEERS * LAYERS
    scores_t, nodes_t = scores.T, nodes.T
    shape = lambda *s: jax.ShapeDtypeStruct(s, F32)

    inputs = [PIN(x) for x in (scores_t, nodes_t, labels[None], bins, pick_feature.T, pick_bin.T)]
    joined, turned, label, target = call(
        join_kernel, "join",
        (
            shape(2 * SHARD, rows), shape(bins.shape[1], HALF), shape(8, HALF),
            jax.ShapeDtypeStruct((8, 128), jnp.int32),
        ),
        [HBM] * 6, inputs,
        scratch=[
            pltpu.VMEM((SHARD, rows), jnp.int32),
            pltpu.VMEM((1, rows), jnp.int32),
            pltpu.VMEM((HALF, bins.shape[1]), jnp.int32),
            pltpu.SMEM((2, NODES, SHARD), jnp.int32),
            pltpu.SemaphoreType.DMA((6,)),
        ],
    )
    every = lax.all_gather(joined, CLS)
    send = call(prepare_kernel, "prepare", shape(LAYERS, 104, HALF), [VMEM] * 3, (every, turned, label))
    came = lax.all_to_all(send, "z", 0, 0)
    send = call(relay_kernel, "relay", shape(PEERS, LAYERS * (BLOCK + 1), HALF), [VMEM], (came,))
    taken = lax.all_to_all(send, ("xl", "xh", "y"), 0, 0, axis_index_groups=neighbours())
    depth = LAYERS * HALF
    buffer = [
        pltpu.VMEM((128, depth), BF16),
        pltpu.VMEM((len(STREAMED) * BINS, depth), BF16),
        pltpu.VMEM((depth, len(TURNED) * BINS), BF16),
    ]
    half = shape(FEATS * BINS // 2, 128)
    own, away = call(
        left_kernel, "left", (half, half), [VMEM], (taken,),
        scratch=[pltpu.VMEM((len(STREAMED) * BINS, 128), F32), pltpu.VMEM((128, len(TURNED) * BINS), F32)] + buffer + buffer, mib=32,
    )
    other = lax.ppermute(away, "core", [(0, 1), (1, 0)])
    pick_feature, pick_bin, own = lax.optimization_barrier((pick_feature, pick_bin, own))
    picks = pick_feature * BINS + pick_bin
    route = call(
        route_kernel, "route", jax.ShapeDtypeStruct((SHARD, rows), jnp.int32), [VMEM] * 3, (picks, nodes_t, bins)
    )
    other, route = lax.optimization_barrier((other, route))
    spread = call(gain_kernel, "gain", shape(chips, 2, 128), [VMEM] * 3, (target, own, other))
    gathered = lax.all_to_all(spread, ROW, 0, 0)
    best, new_scores = call(
        finish_kernel, "finish", (shape(NODES, SHARD), shape(SHARD, rows)), [VMEM] * 3, (gathered, scores_t, route)
    )
    return best.T, new_scores.T


def solution(mesh):
    fine = Mesh(mesh.devices.reshape(2, 2, 2, LAYERS, COLUMNS), CLS + ROW)
    in_specs = (P(ROW, CLS), P(ROW), P(ROW, CLS), P(ROW, None), P(CLS, None), P(CLS, None))
    out_specs = (P(CLS, None), P(ROW, CLS))
    return jax.shard_map(per_device, mesh=fine, in_specs=in_specs, out_specs=out_specs, check_vma=False)
```
